256 devices in a mesh: comp: 64 (over z, y, x_lo), band: 4 (over x_hi, core).
Axes of the slice: x: 4 (x_hi: 2, x_lo: 2; x = x_hi * 2 + x_lo), y: 4, z: 8, core: 2. Of those that a mesh axis runs over, the one named last changes fastest.
Arguments:
- spectrum: float32 [1152, 32, 4096], P('comp', 'band'), may hold values from 0.1 to 1
- currents: float32 [2, 32, 4096], P(None, 'band', 'comp'), may hold values from -4 to 4
- group_courant: float32 [32], replicated, may hold values from 0.1 to 0.35
- refraction: float32 [8, 32], replicated, may hold values from -0.25 to 0.25
- interp: float32 [1152, 1152], replicated, may hold values from -0.1875 to 0.1875
- sea_mask: int32 [32, 4096], replicated, may hold values 0 or 1
- depth_class: int32 [32, 4096], replicated, may hold values from 0 to 7
- owner_map: int32 [64], replicated, may hold values from 0 to 63, each once
Outputs:
- spectrum_out: float32 [1152, 32, 4096], P('comp', 'band')
- ocean_out: float32 [2, 32, 4096], P(None, 'band', 'comp')
The draws below stay inside these ranges and needn't reach their ends.
Inputs may be any that keep to these rules, and one draw needn't show every extreme that they name: `owner_map`: each of 0 to 63 once.
All inputs are finite; a program needn't handle non-finite values.
Results may differ from the reference program's by a relative error of at most 0.000098.
Values sent between devices are 32-bit elements; how exact they have to be, the bound alone decides.
A program may use at most 128 MiB of HBM per device.

```python
import math
import jax
import jax.numpy as jnp
from jax import lax

DIRS = 36
FREQ = 32
CLASSES = 8
SUBSTEPS = 4
LON = 4096
COMPS = 1152
ROWS = 32
TILES = 64


def place_ends(values, own_key, least, largest):
    dims = values.shape
    place = [jax.random.randint(jax.random.fold_in(own_key, axis), (), 0, dims[axis]) for axis in range(len(dims))]
    values = values.at[tuple(place)].set(least)
    longest = dims.index(max(dims))
    place[longest] = (place[longest] + 1) % dims[longest]
    return values.at[tuple(place)].set(largest)


def shard_levels(key, dims, cuts, low, largest):
    def one(position, shards_of):
        heights = jax.random.uniform(jax.random.fold_in(jax.random.fold_in(key, 6), position), (shards_of,), jnp.float32, low / len(cuts), largest / len(cuts))
        return jnp.repeat(jnp.exp(heights), dims[position] // shards_of).reshape((-1,) + (1,) * (len(dims) - position - 1))

    level = one(*cuts[0])
    for cut in cuts[1:]:
        level = level * one(*cut)
    return level


def scatter_about(stream_key, shape, spread, most, shards=(), held_as=jnp.bfloat16):
    array = spread * jax.random.normal(stream_key, shape, jnp.float32)
    if shards:
        array = array * shard_levels(stream_key, shape, shards, -0.22, 0.18)
    return jnp.clip(array, -most, most).astype(held_as)


def setup_inputs(seed: int = 0) -> dict:
    splits = jax.random.split(jax.random.key(seed), 9)
    return {
        "spectrum": jnp.clip(jnp.exp(math.log(1.0) - 2.3025851 * jax.random.uniform(splits[0], (COMPS, ROWS, LON), jnp.float32) ** shard_levels(splits[0], (COMPS, ROWS, LON), ((0, 64), (1, 4)), -0.2, 0.2)), 0.1, 1.0),
        "currents": scatter_about(splits[1], (2, ROWS, LON), 1.0, 4.0, ((1, 4), (2, 64)), jnp.float32),
        "group_courant": jnp.clip(jnp.exp(jax.random.uniform(splits[2], (FREQ,), jnp.float32, math.log(0.1), math.log(0.35))), 0.1, 0.35),
        "refraction": jnp.clip(jax.random.uniform(splits[3], (CLASSES, FREQ), jnp.float32, -0.25, 0.25), -0.25, 0.25),
        "interp": scatter_about(splits[4], (COMPS, COMPS), COMPS ** -0.5, 0.1875, (), jnp.float32),
        "sea_mask": place_ends((jax.random.randint(splits[5], (ROWS, LON), 0, 4) < 3).astype(jnp.int32), jax.random.fold_in(splits[5], 1), 0, 1),
        "depth_class": place_ends(jax.random.randint(splits[6], (ROWS, LON), 0, CLASSES), jax.random.fold_in(splits[6], 1), 0, CLASSES - 1).astype(jnp.int32),
        "owner_map": jax.random.permutation(splits[7], TILES).astype(jnp.int32),
    }


CURRENT_COURANT = 0.025
SOURCE_STEP = 0.5
STOKES_SCALE = 0.2
OCEAN_STEP = 0.5
VISCOSITY = 0.2
DRAG = 0.1
HIGHEST = lax.Precision.HIGHEST


def reorder_tiles(values_in, tile_order, tile_count):
    lead_dim, row_count, col_count = values_in.shape
    pieces = values_in.reshape(lead_dim, row_count, tile_count, col_count // tile_count)
    return jnp.take(pieces, tile_order, axis=2).reshape(lead_dim, row_count, col_count)


def upwind(centre_val, behind, ahead_val, speeds):
    return jnp.maximum(speeds, 0.0) * (centre_val - behind) + jnp.minimum(speeds, 0.0) * (ahead_val - centre_val)


def stokes_weights():
    component = jnp.arange(COMPS, dtype=jnp.int32)
    frequency = component // DIRS
    direction = component % DIRS
    angles = direction.astype(jnp.float32) * (2.0 * math.pi / DIRS)
    scales = STOKES_SCALE * (frequency + 1).astype(jnp.float32) / FREQ
    return jnp.stack([scales * jnp.cos(angles), scales * jnp.sin(angles)])


def reference(spectrum, currents, group_courant, refraction, interp, sea_mask, depth_class, owner_map):
    ocean_field = sea_mask.astype(jnp.float32)
    inverse = jnp.argsort(owner_map).astype(jnp.int32)
    current_real = reorder_tiles(currents, inverse, TILES)
    direction = jnp.arange(DIRS, dtype=jnp.int32)
    angles = direction.astype(jnp.float32) * (2.0 * math.pi / DIRS)
    cosine = jnp.cos(angles)[:, None, None]
    sines = jnp.sin(angles)[:, None, None]
    lon_base = CURRENT_COURANT * current_real[0]
    lat_base = CURRENT_COURANT * current_real[1]

    def one_frequency(inputs):
        wave_block, speeds, table = inputs
        lon_speed = speeds * cosine + lon_base[None]
        lat_speed = speeds * sines + lat_base[None]
        turning = jnp.take(table, depth_class)
        dir_speed = turning[None] * cosine
        for substep in range(SUBSTEPS):
            padded = jnp.pad(wave_block, ((0, 0), (1, 1), (0, 0)))
            centre = padded[:, 1:-1]
            south_rows = padded[:, :-2]
            north_rows = padded[:, 2:]
            west_cols = jnp.roll(centre, 1, axis=2)
            east_cols = jnp.roll(centre, -1, axis=2)
            before_dir = jnp.roll(centre, 1, axis=0)
            after_dir = jnp.roll(centre, -1, axis=0)
            change = upwind(centre, west_cols, east_cols, lon_speed) + upwind(centre, south_rows, north_rows, lat_speed) + upwind(centre, before_dir, after_dir, dir_speed)
            wave_block = ocean_field[None] * (centre - change)
        return wave_block

    blocks = (spectrum * ocean_field[None]).reshape(FREQ, DIRS, ROWS, LON)
    wave_state = lax.map(one_frequency, (blocks, group_courant, jnp.transpose(refraction)))
    flat_state = wave_state.reshape(COMPS, ROWS, LON)
    weights = stokes_weights()

    def one_row(row_index):
        wave_row = lax.dynamic_index_in_dim(flat_state, row_index, 1, keepdims=False)
        forward = jnp.dot(interp, wave_row, precision=HIGHEST, preferred_element_type=jnp.float32)
        backward = jnp.dot(jnp.transpose(interp), wave_row, precision=HIGHEST, preferred_element_type=jnp.float32)
        updated = wave_row + SOURCE_STEP * (forward * backward - 0.5 * wave_row * (forward + backward))
        drift_row = jnp.dot(weights, updated, precision=HIGHEST, preferred_element_type=jnp.float32)
        return updated, drift_row

    updated_rows, drift_rows = lax.map(one_row, jnp.arange(ROWS, dtype=jnp.int32))
    spectrum_out = jnp.moveaxis(updated_rows, 0, 1)
    stokes = jnp.moveaxis(drift_rows, 0, 1)

    masked_cur = current_real * ocean_field[None]
    padded_cur = jnp.pad(masked_cur, ((0, 0), (1, 1), (0, 0)))
    laplace = jnp.roll(masked_cur, 1, axis=2) + jnp.roll(masked_cur, -1, axis=2) + padded_cur[:, :-2] + padded_cur[:, 2:] - 4.0 * masked_cur
    latitude = -1.2 + 2.4 * (jnp.arange(ROWS, dtype=jnp.int32).astype(jnp.float32) + 0.5) / ROWS
    coriolis = jnp.sin(latitude)[:, None]
    east_new = ocean_field * (masked_cur[0] + OCEAN_STEP * (coriolis * (masked_cur[1] + stokes[1]) + VISCOSITY * laplace[0] - DRAG * masked_cur[0]))
    north_new = ocean_field * (masked_cur[1] + OCEAN_STEP * (-coriolis * (masked_cur[0] + stokes[0]) + VISCOSITY * laplace[1] - DRAG * masked_cur[1]))
    ocean_out = reorder_tiles(jnp.stack([east_new, north_new]), owner_map, TILES)
    return spectrum_out, ocean_out
```

```python
import math

import jax
import jax.numpy as jnp
import numpy as np
from jax import lax
from jax.experimental import pallas as pl
from jax.experimental.pallas import tpu as pltpu
from jax.sharding import PartitionSpec as P

DIRS = 36
FREQ = 32
CLASSES = 8
SUBSTEPS = 4
COMPS = 1152
OWN = 18
ROWS = 8
TOTAL_ROWS = 32
LON = 4096
TILES = 64
PLANE = 8
LANES = 128
BLOCK = OWN * 4
CHUNK = 144
POINTS = 512
PIECE = 1024
MESH = pl.DeviceIdType.MESH
f32 = jnp.float32
bf16 = jnp.bfloat16


def plane_offset(step):
    return 4 + (1 - 2 * (step % 2)) * ((step + 1) // 2)


def wave_kernel(
    spectrum, cat, sea, classes, interp_any, weights, courant, refraction, inverse, cosine, sine,
    recv2, drift_all, gathered, beside,
    state, rows_out, rows_in, base_u, base_v, turning, ocean, send1, recv1, interp, interp_t, split,
    points, points_hi, points_lo, drift_block,
    interp_sem, cur_send, cur_recv, beside_send, beside_recv, edge_send, edge_recv,
    in_send, in_recv, out_send, out_recv, drift_send, drift_recv, own_sem,
):
    me = lax.axis_index("comp")
    band = lax.axis_index("band")
    plane = me // PLANE
    low = me % PLANE
    partner = me + 1 - 2 * (me % 2)
    freq = me // 2
    first_dir = (me % 2) * OWN
    south = band > 0
    north = band < 3

    load_interp = pltpu.make_async_copy(interp_any, interp, interp_sem)
    load_interp.start()

    barrier = pltpu.get_barrier_semaphore()

    @pl.loop(1, TILES)
    def _(t):
        pl.semaphore_signal(barrier, inc=1, device_id={"comp": (me + t) % TILES}, device_id_type=MESH)

    @pl.when(south)
    def _():
        pl.semaphore_signal(barrier, inc=1, device_id={"band": band - 1}, device_id_type=MESH)

    @pl.when(north)
    def _():
        pl.semaphore_signal(barrier, inc=1, device_id={"band": band + 1}, device_id_type=MESH)

    rows8 = pl.ds(pl.multiple_of(band * ROWS, ROWS), ROWS)
    ocean[...] = sea[rows8, :].astype(f32)

    def row_copy(side, step):
        return pltpu.make_async_remote_copy(
            src_ref=rows_out.at[step, side],
            dst_ref=rows_in.at[step, side],
            send_sem=edge_send.at[step, side],
            recv_sem=edge_recv.at[step, side],
            device_id={"band": band + 1 - 2 * side},
            device_id_type=MESH,
        )

    def dir_copy(side, step):
        return pltpu.make_async_remote_copy(
            src_ref=state.at[step, OWN if side == 0 else 1],
            dst_ref=state.at[step, 0 if side == 0 else OWN + 1],
            send_sem=edge_send.at[step, 2 + side],
            recv_sem=edge_recv.at[step, 2 + side],
            device_id={"comp": partner},
            device_id_type=MESH,
        )

    def start_edges(step):
        dir_copy(0, step).start()
        dir_copy(1, step).start()

        @pl.when(north)
        def _():
            row_copy(0, step).start()

        @pl.when(south)
        def _():
            row_copy(1, step).start()

    def finish_edges(step):
        for side in range(2):
            dir_copy(side, step).wait_recv()
            dir_copy(side, step).wait_send()

        @pl.when(south)
        def _():
            row_copy(0, step).wait_recv()
            row_copy(1, step).wait_send()

        @pl.when(north)
        def _():
            row_copy(1, step).wait_recv()
            row_copy(0, step).wait_send()

    @pl.loop(0, OWN)
    def _(i):
        masked = spectrum[i] * ocean[...]
        state[0, i + 1] = masked
        rows_out[0, 0, i] = masked[ROWS - 1 :, :]
        rows_out[0, 1, i] = masked[:1, :]

    pl.semaphore_wait(barrier, TILES - 1 + jnp.where(south, 1, 0) + jnp.where(north, 1, 0))

    def cur_copy(t):
        return pltpu.make_async_remote_copy(
            src_ref=cat,
            dst_ref=gathered.at[me],
            send_sem=cur_send.at[t],
            recv_sem=cur_recv.at[t],
            device_id={"comp": (me + t) % TILES},
            device_id_type=MESH,
        )

    def beside_copy(side):
        return pltpu.make_async_remote_copy(
            src_ref=cat,
            dst_ref=beside.at[side],
            send_sem=beside_send.at[side],
            recv_sem=beside_recv.at[side],
            device_id={"band": band + 1 - 2 * side},
            device_id_type=MESH,
        )

    @pl.loop(1, TILES)
    def _(t):
        cur_copy(t).start()

    start_edges(0)

    @pl.when(north)
    def _():
        beside_copy(0).start()

    @pl.when(south)
    def _():
        beside_copy(1).start()

    gathered[me] = cat[...]

    @pl.when(band == 0)
    def _():
        rows_in[:, 0] = jnp.zeros((SUBSTEPS, OWN, 1, LON), f32)

    @pl.when(band == 3)
    def _():
        rows_in[:, 1] = jnp.zeros((SUBSTEPS, OWN, 1, LON), f32)

    own_class = classes[rows8, :]
    turned = jnp.zeros((ROWS, LON), f32)
    for level in range(CLASSES):
        turned = jnp.where(own_class == level, refraction[level, freq], turned)
    turning[...] = turned

    @pl.loop(1, TILES)
    def _(t):
        cur_copy(t).wait_recv()

    lane = lax.broadcasted_iota(jnp.int32, (ROWS, LANES), 1)
    for u in range(TILES // 2):
        one = gathered[inverse[2 * u]]
        two = gathered[inverse[2 * u + 1]]
        at = slice(u * LANES, (u + 1) * LANES)
        base_u[:, at] = 0.025 * jnp.where(lane < 64, one, pltpu.roll(two, 64, 1))
        base_v[:, at] = 0.025 * jnp.where(lane < 64, pltpu.roll(one, 64, 1), two)

    row = lax.broadcasted_iota(jnp.int32, (ROWS, PIECE), 0)
    speed = courant[freq]

    def advanced(step, i, piece):
        lo = piece * PIECE
        at = slice(lo, lo + PIECE)
        centre = state[step, i + 1, :, at]
        if piece == 0:
            west_piece = state[step, i + 1, :, LON - LANES :]
        else:
            west_piece = state[step, i + 1, :, lo - LANES : lo]
        if piece == LON // PIECE - 1:
            east_piece = state[step, i + 1, :, :LANES]
        else:
            east_piece = state[step, i + 1, :, lo + PIECE : lo + PIECE + LANES]
        wide = jnp.concatenate([west_piece, centre, east_piece], axis=1)
        west = pltpu.roll(wide, 1, 1)[:, LANES:-LANES]
        east = pltpu.roll(wide, PIECE + 2 * LANES - 1, 1)[:, LANES:-LANES]
        below = jnp.where(row == 0, rows_in[step, 0, i, :, at], pltpu.roll(centre, 1, 0))
        above = jnp.where(row == ROWS - 1, rows_in[step, 1, i, :, at], pltpu.roll(centre, ROWS - 1, 0))
        before = state[step, i, :, at]
        after = state[step, i + 2, :, at]
        cos_d = cosine[first_dir + i]
        ax = base_u[:, at] + speed * cos_d
        ay = base_v[:, at] + speed * sine[first_dir + i]
        turn = turning[:, at] * cos_d
        change = (
            jnp.maximum(ax, 0.0) * (centre - west) + jnp.minimum(ax, 0.0) * (east - centre)
            + (jnp.maximum(ay, 0.0) * (centre - below) + jnp.minimum(ay, 0.0) * (above - centre))
            + (jnp.maximum(turn, 0.0) * (centre - before) + jnp.minimum(turn, 0.0) * (after - centre))
        )
        return ocean[:, at] * (centre - change)

    for step in range(SUBSTEPS - 1):
        finish_edges(step)

        @pl.loop(0, OWN)
        def _(i):
            for piece in range(LON // PIECE):
                at = slice(piece * PIECE, (piece + 1) * PIECE)
                new = advanced(step, i, piece)
                state[step + 1, i + 1, :, at] = new
                rows_out[step + 1, 0, i, :, at] = new[ROWS - 1 :, :]
                rows_out[step + 1, 1, i, :, at] = new[:1, :]

        start_edges(step + 1)

    finish_edges(SUBSTEPS - 1)

    @pl.loop(0, OWN)
    def _(i):
        for piece in range(LON // PIECE):
            new = advanced(SUBSTEPS - 1, i, piece)
            for tile in range(PIECE // LANES):
                col = piece * (PIECE // LANES) + tile
                first = (col // 4) * ROWS * BLOCK + col % 4
                send1[pl.ds(first + i * 4, ROWS, stride=BLOCK), :] = new[:, tile * LANES : (tile + 1) * LANES]

    def block_of(ref, owner):
        return ref.at[pl.ds(pl.multiple_of(owner * BLOCK, 8), BLOCK)]

    def in_copy(k):
        to = ((plane + plane_offset(k // PLANE)) % PLANE) * PLANE + (low + k % PLANE) % PLANE
        return pltpu.make_async_remote_copy(
            src_ref=block_of(send1, to),
            dst_ref=block_of(recv1, me),
            send_sem=in_send.at[k],
            recv_sem=in_recv.at[k],
            device_id={"comp": to},
            device_id_type=MESH,
        )

    @pl.loop(0, 56)
    def _(k):
        in_copy(k).start()

    @pl.loop(57, TILES)
    def _(k):
        in_copy(k).start()

    own_rows = pl.ds(pl.multiple_of(me * BLOCK, 8), BLOCK)
    recv1[own_rows, :] = send1[own_rows, :]

    load_interp.wait()

    @pl.loop(0, COMPS // LANES)
    def _(b):
        cols = pl.ds(pl.multiple_of(b * LANES, LANES), LANES)
        interp_t[cols, :] = interp[:, cols].T

    @pl.loop(0, COMPS // CHUNK)
    def _(c):
        rows = pl.ds(pl.multiple_of(c * CHUNK, 16), CHUNK)
        for part, source in enumerate((interp, interp_t)):
            value = source[rows, :]
            high = value.astype(bf16)
            split[c, part * CHUNK : (part + 1) * CHUNK, :] = high
            split[c, (2 + part) * CHUNK : (3 + part) * CHUNK, :] = (value - high.astype(f32)).astype(bf16)

    @pl.loop(0, 56)
    def _(k):
        in_copy(k).wait_recv()

    @pl.loop(57, TILES)
    def _(k):
        in_copy(k).wait_recv()

    @pl.loop(0, COMPS // CHUNK)
    def _(c):
        rows = pl.ds(pl.multiple_of(c * CHUNK, 16), CHUNK)
        for q in range(4):
            value = recv1[pl.ds(c * (CHUNK * 4) + q, CHUNK, stride=4), :]
            at = slice(q * LANES, (q + 1) * LANES)
            high = value.astype(bf16)
            points[rows, at] = value
            points_hi[rows, at] = high
            points_lo[rows, at] = (value - high.astype(f32)).astype(bf16)

    @pl.loop(0, 56)
    def _(k):
        in_copy(k).wait_send()

    @pl.loop(57, TILES)
    def _(k):
        in_copy(k).wait_send()

    def out_copy(to):
        return pltpu.make_async_remote_copy(
            src_ref=block_of(send1, to),
            dst_ref=block_of(recv2, me),
            send_sem=out_send.at[to],
            recv_sem=out_recv.at[me],
            device_id={"comp": to},
            device_id_type=MESH,
        )

    own_copy = pltpu.make_async_copy(block_of(send1, me), block_of(recv2, me), own_sem)

    def source_chunk(c, drift):
        group = (plane + plane_offset(c)) % PLANE
        rows = pl.ds(pl.multiple_of(group * CHUNK, 16), CHUNK)
        both = jnp.dot(split[group], points_hi[...], preferred_element_type=f32)
        more = jnp.dot(split[group, : 2 * CHUNK, :], points_lo[...], preferred_element_type=f32)
        sums = both[: 2 * CHUNK] + (both[2 * CHUNK :] + more)
        forward, backward = sums[:CHUNK], sums[CHUNK:]
        wave = points[rows, :]
        new = wave + 0.5 * (forward * backward - 0.5 * wave * (forward + backward))
        for q in range(4):
            send1[pl.ds(group * (CHUNK * 4) + q, CHUNK, stride=4), :] = new[:, q * LANES : (q + 1) * LANES]

        @pl.loop(0, PLANE)
        def _(e):
            to = group * PLANE + (low + e) % PLANE

            @pl.when(to != me)
            def _():
                out_copy(to).start()

        held = weights[rows, :]
        return tuple(
            drift[a] + jnp.sum((held[:, a : a + 1] * new).reshape(CHUNK // 8, 8, POINTS), axis=0) for a in range(2)
        )

    drift = lax.fori_loop(
        0, PLANE, source_chunk, (jnp.zeros((8, POINTS), f32), jnp.zeros((8, POINTS), f32))
    )
    own_copy.start()
    for a in range(2):
        total = jnp.sum(drift[a], axis=0, keepdims=True)
        for q in range(4):
            drift_block[a * 4 + q : a * 4 + q + 1, :] = total[:, q * LANES : (q + 1) * LANES]

    def drift_copy(t):
        return pltpu.make_async_remote_copy(
            src_ref=drift_block,
            dst_ref=drift_all.at[pl.ds(pl.multiple_of(me * 8, 8), 8)],
            send_sem=drift_send.at[t],
            recv_sem=drift_recv.at[t],
            device_id={"comp": (me + t) % TILES},
            device_id_type=MESH,
        )

    @pl.loop(1, TILES)
    def _(t):
        drift_copy(t).start()

    drift_all[pl.ds(pl.multiple_of(me * 8, 8), 8), :] = drift_block[...]

    @pl.loop(1, TILES)
    def _(t):
        other = (me + t) % TILES
        cur_copy(t).wait_send()
        out_copy(other).wait_send()
        pltpu.make_async_remote_copy(
            src_ref=block_of(send1, other),
            dst_ref=block_of(recv2, other),
            send_sem=out_send.at[other],
            recv_sem=out_recv.at[other],
            device_id={"comp": other},
            device_id_type=MESH,
        ).wait_recv()
        drift_copy(t).wait()

    own_copy.wait()

    @pl.when(north)
    def _():
        beside_copy(0).wait_send()
        beside_copy(1).wait_recv()

    @pl.when(south)
    def _():
        beside_copy(1).wait_send()
        beside_copy(0).wait_recv()


def finish_kernel(blocks, drift_all, gathered, beside, cat, sea, coriolis, owner, inverse, place, out, ocean_out):
    @pl.loop(0, OWN)
    def _(i):
        for col in range(LON // LANES):
            first = (col // 4) * ROWS * BLOCK + col % 4
            out[i, :, col * LANES : (col + 1) * LANES] = blocks[pl.ds(first + i * 4, ROWS, stride=BLOCK), :]

    me, band = place[0], place[1]
    tile = owner[me]
    lane = lax.broadcasted_iota(jnp.int32, (ROWS, LANES), 1)
    row = lax.broadcasted_iota(jnp.int32, (ROWS, LANES), 0)
    left = lane < 64

    def twice(value, half):
        other = pltpu.roll(value, 64, 1)
        mine = jnp.where(half == 0, value, other)
        return mine, jnp.where(half == 0, other, value)

    def mask(which_tile, which_band):
        rows = pl.ds(pl.multiple_of(which_band * ROWS, ROWS), ROWS)
        cols = pl.ds(pl.multiple_of((which_tile // 2) * LANES, LANES), LANES)
        at_left, at_right = twice(sea[rows, cols].astype(f32), which_tile % 2)
        return jnp.where(left, at_left, at_right)

    own = mask(tile, band)
    held = cat[...] * own
    west_tile, east_tile = (tile + TILES - 1) % TILES, (tile + 1) % TILES
    held_w = gathered[inverse[west_tile]] * mask(west_tile, band)
    held_e = gathered[inverse[east_tile]] * mask(east_tile, band)
    held_s = jnp.where(band > 0, beside[0] * mask(tile, jnp.maximum(band - 1, 0)), 0.0)
    held_n = jnp.where(band < 3, beside[1] * mask(tile, jnp.minimum(band + 1, 3)), 0.0)
    west = jnp.where(lane % 64 == 0, pltpu.roll(held_w, 65, 1), pltpu.roll(held, 1, 1))
    east = jnp.where(lane % 64 == 63, pltpu.roll(held_e, 63, 1), pltpu.roll(held, 127, 1))
    below = jnp.where(row == 0, pltpu.roll(held_s, 1, 0), pltpu.roll(held, 1, 0))
    above = jnp.where(row == ROWS - 1, pltpu.roll(held_n, 7, 0), pltpu.roll(held, 7, 0))
    lap = west + east + below + above - 4.0 * held
    first = (tile // 8) * 64 + (tile % 8) // 2
    eastward, _ = twice(drift_all[pl.ds(first, ROWS, stride=8), :], tile % 2)
    _, northward = twice(drift_all[pl.ds(first + 4, ROWS, stride=8), :], tile % 2)
    stokes = jnp.where(left, eastward, northward)
    rows8 = pl.ds(pl.multiple_of(band * ROWS, ROWS), ROWS)
    turn = jnp.where(left, 1.0, -1.0) * coriolis[rows8, :]
    other = pltpu.roll(held + stokes, 64, 1)
    ocean_out[...] = own * (held + 0.5 * (turn * other + 0.2 * lap - 0.1 * held))


def tables():
    angles = np.arange(DIRS, dtype=np.float32) * np.float32(2.0 * math.pi / DIRS)
    cosine, sine = np.cos(angles).astype(np.float32), np.sin(angles).astype(np.float32)
    k = np.arange(COMPS)
    scale = (np.float32(0.2) * (k // DIRS + 1).astype(np.float32) / np.float32(FREQ)).astype(np.float32)
    weights = np.stack([scale * cosine[k % DIRS], scale * sine[k % DIRS]], axis=1)
    latitude = -1.2 + 2.4 * (np.arange(TOTAL_ROWS, dtype=np.float32) + np.float32(0.5)) / TOTAL_ROWS
    coriolis = np.broadcast_to(np.sin(latitude.astype(np.float32))[:, None], (TOTAL_ROWS, LANES))
    return cosine, sine, weights.astype(np.float32), coriolis.astype(np.float32)


def local(spectrum, currents, group_courant, refraction, interp, sea_mask, depth_class, owner_map):
    cosine, sine, weights, coriolis = tables()
    cat = jnp.concatenate([currents[0], currents[1]], axis=1)
    index = jnp.arange(TILES, dtype=jnp.int32)
    inverse = jnp.sum(jnp.where(owner_map[None, :] == index[:, None], index[None, :], 0), axis=1)
    place = jnp.stack([lax.axis_index("comp"), lax.axis_index("band")]).astype(jnp.int32)
    vmem, smem = pl.BlockSpec(memory_space=pltpu.VMEM), pl.BlockSpec(memory_space=pltpu.SMEM)
    anywhere = pl.BlockSpec(memory_space=pl.ANY)
    dma = pltpu.SemaphoreType.DMA
    wide = (ROWS, LON)
    blocks, drift_all, gathered, beside = pl.pallas_call(
        wave_kernel,
        out_shape=(
            jax.ShapeDtypeStruct((TILES * BLOCK, LANES), f32),
            jax.ShapeDtypeStruct((TILES * 8, LANES), f32),
            jax.ShapeDtypeStruct((TILES, ROWS, LANES), f32),
            jax.ShapeDtypeStruct((2, ROWS, LANES), f32),
        ),
        in_specs=[vmem, vmem, vmem, vmem, anywhere, vmem, smem, smem, smem, smem, smem],
        out_specs=(anywhere, vmem, vmem, vmem),
        scratch_shapes=[
            pltpu.VMEM((SUBSTEPS, OWN + 2, ROWS, LON), f32),
            pltpu.VMEM((SUBSTEPS, 2, OWN, 1, LON), f32),
            pltpu.VMEM((SUBSTEPS, 2, OWN, 1, LON), f32),
            pltpu.VMEM(wide, f32),
            pltpu.VMEM(wide, f32),
            pltpu.VMEM(wide, f32),
            pltpu.VMEM(wide, f32),
            pltpu.VMEM((TILES * BLOCK, LANES), f32),
            pltpu.VMEM((TILES * BLOCK, LANES), f32),
            pltpu.VMEM((COMPS, COMPS), f32),
            pltpu.VMEM((COMPS, COMPS), f32),
            pltpu.VMEM((COMPS // CHUNK, 4 * CHUNK, COMPS), bf16),
            pltpu.VMEM((COMPS, POINTS), f32),
            pltpu.VMEM((COMPS, POINTS), bf16),
            pltpu.VMEM((COMPS, POINTS), bf16),
            pltpu.VMEM((8, LANES), f32),
            dma,
            dma((TILES,)),
            dma((TILES,)),
            dma((2,)),
            dma((2,)),
            dma((SUBSTEPS, 4)),
            dma((SUBSTEPS, 4)),
            dma((TILES,)),
            dma((TILES,)),
            dma((TILES,)),
            dma((TILES,)),
            dma((TILES,)),
            dma((TILES,)),
            dma,
        ],
        compiler_params=pltpu.CompilerParams(
            collective_id=0, has_side_effects=True, vmem_limit_bytes=60 * 2**20
        ),
        name="waves",
    )(
        spectrum, cat, sea_mask, depth_class, interp, jnp.asarray(weights), group_courant, refraction, inverse,
        jnp.asarray(cosine), jnp.asarray(sine),
    )
    out, ocean_cat = pl.pallas_call(
        finish_kernel,
        out_shape=(
            jax.ShapeDtypeStruct((OWN, ROWS, LON), f32),
            jax.ShapeDtypeStruct((ROWS, LANES), f32),
        ),
        in_specs=[vmem] * 7 + [smem] * 3,
        out_specs=(vmem, vmem),
        compiler_params=pltpu.CompilerParams(vmem_limit_bytes=32 * 2**20),
        name="finish",
    )(
        blocks, drift_all, gathered, beside, cat, sea_mask, jnp.asarray(coriolis), owner_map, inverse, place,
    )
    ocean_out = jnp.stack([ocean_cat[:, :64], ocean_cat[:, 64:]])
    return out, ocean_out


def solution(mesh):
    in_specs = (P("comp", "band", None), P(None, "band", "comp"), P(), P(), P(), P(), P(), P())
    out_specs = (P("comp", "band", None), P(None, "band", "comp"))
    return jax.shard_map(local, mesh=mesh, in_specs=in_specs, out_specs=out_specs, check_vma=False)
```

```python
import math

import jax
import jax.numpy as jnp
import numpy as np
from jax import lax
from jax.experimental import pallas as pl
from jax.experimental.pallas import tpu as pltpu
from jax.sharding import PartitionSpec as P

DIRS = 36
FREQ = 32
CLASSES = 8
SUBSTEPS = 4
COMPS = 1152
OWN = 18
ROWS = 8
TOTAL_ROWS = 32
LON = 4096
TILES = 64
PLANE = 8
LANES = 128
BLOCK = OWN * 4
CHUNK = 144
POINTS = 512
HALF = 2048
REGION = HALF + 2 * LANES
PIECE = 1152
MESH = pl.DeviceIdType.MESH
f32 = jnp.float32
bf16 = jnp.bfloat16


def plane_offset(step):
    return 4 + (1 - 2 * (step % 2)) * ((step + 1) // 2)


def order_of(device):
    return (device // 2) % 2 * (TILES // 2) + device // 4 * 2 + device % 2


def block_of(ref, which):
    return ref.at[pl.ds(pl.multiple_of(which * BLOCK, 8), BLOCK)]


def wait_bytes(ref, sem):
    pltpu.make_async_copy(ref, ref, sem).wait()


def wave_kernel(
    spectrum, currents, sea, classes, interp_any, weights, coriolis, courant, refraction, owner, inverse, cosine, sine,
    out_any, ocean_out,
    state, rows_out, rows_in, base_u, base_v, turning, ocean, send1, recv1, send2, recv2, out, interp, split,
    points, points_hi, points_lo, cat, gathered, beside, drift_block, drift_all, masks,
    interp_sem, cur_send, cur_recv, beside_send, beside_recv, edge_send, edge_recv,
    in_send, in_recv, out_send, out_recv, drift_send, drift_recv, store_sem,
):
    me = lax.axis_index("comp")
    band = lax.axis_index("band")
    plane = me // PLANE
    low = me % PLANE
    partner = me + 1 - 2 * (me % 2)
    freq = me // 2
    first_dir = (me % 2) * OWN
    my_order = order_of(me)
    south = band > 0
    north = band < 3

    load_interp = pltpu.make_async_copy(interp_any, interp, interp_sem)
    load_interp.start()

    barrier = pltpu.get_barrier_semaphore()

    @pl.loop(1, TILES)
    def _(t):
        pl.semaphore_signal(barrier, inc=1, device_id={"comp": (me + t) % TILES}, device_id_type=MESH)

    @pl.when(south)
    def _():
        pl.semaphore_signal(barrier, inc=1, device_id={"band": band - 1}, device_id_type=MESH)

    @pl.when(north)
    def _():
        pl.semaphore_signal(barrier, inc=1, device_id={"band": band + 1}, device_id_type=MESH)

    rows8 = pl.ds(pl.multiple_of(band * ROWS, ROWS), ROWS)

    def store_wrapped(ref, value):
        ref[:, LANES : LANES + LON] = value
        ref[:, :LANES] = value[:, LON - LANES :]
        ref[:, LANES + LON :] = value[:, :LANES]

    store_wrapped(ocean, sea[rows8, :].astype(f32))
    cat[:, :64] = currents[0]
    cat[:, 64:] = currents[1]

    def row_copy(half, side, step):
        return pltpu.make_async_remote_copy(
            src_ref=rows_out.at[half, step, side],
            dst_ref=rows_in.at[half, step, side],
            send_sem=edge_send.at[half, step, side],
            recv_sem=edge_recv.at[half, step, side],
            device_id={"band": band + 1 - 2 * side},
            device_id_type=MESH,
        )

    def dir_copy(half, side, step):
        return pltpu.make_async_remote_copy(
            src_ref=state.at[half, step, OWN if side == 0 else 1],
            dst_ref=state.at[half, step, 0 if side == 0 else OWN + 1],
            send_sem=edge_send.at[half, step, 2 + side],
            recv_sem=edge_recv.at[half, step, 2 + side],
            device_id={"comp": partner},
            device_id_type=MESH,
        )

    def start_edges(half, step):
        @pl.when(north)
        def _():
            row_copy(half, 0, step).start()

        @pl.when(south)
        def _():
            row_copy(half, 1, step).start()

        dir_copy(half, 0, step).start()
        dir_copy(half, 1, step).start()

    def finish_edges(half, step):
        for side in range(2):
            dir_copy(half, side, step).wait_recv()
            dir_copy(half, side, step).wait_send()

        @pl.when(south)
        def _():
            row_copy(half, 0, step).wait_recv()
            row_copy(half, 1, step).wait_send()

        @pl.when(north)
        def _():
            row_copy(half, 1, step).wait_recv()
            row_copy(half, 0, step).wait_send()

    def first_state(half):
        start = half * HALF
        west = (start - LANES) % LON
        east = (start + HALF) % LON

        @pl.loop(0, OWN)
        def _(i):
            for to, source, length in ((0, west, LANES), (LANES, start, HALF), (LANES + HALF, east, LANES)):
                masked = spectrum[i, :, source : source + length] * ocean[:, start + to : start + to + length]
                state[half, 0, i + 1, :, to : to + length] = masked
                rows_out[half, 0, 0, i, :, to : to + length] = masked[ROWS - 1 :, :]
                rows_out[half, 0, 1, i, :, to : to + length] = masked[:1, :]

    first_state(0)
    pl.semaphore_wait(barrier, TILES - 1 + jnp.where(south, 1, 0) + jnp.where(north, 1, 0))

    def cur_copy(t):
        return pltpu.make_async_remote_copy(
            src_ref=cat,
            dst_ref=gathered.at[me],
            send_sem=cur_send,
            recv_sem=cur_recv,
            device_id={"comp": (me + t) % TILES},
            device_id_type=MESH,
        )

    def beside_copy(side):
        return pltpu.make_async_remote_copy(
            src_ref=cat,
            dst_ref=beside.at[side],
            send_sem=beside_send.at[side],
            recv_sem=beside_recv.at[side],
            device_id={"band": band + 1 - 2 * side},
            device_id_type=MESH,
        )

    start_edges(0, 0)

    @pl.loop(1, TILES)
    def _(t):
        cur_copy(t).start()

    pltpu.make_async_copy(cat, gathered.at[me], cur_recv).start()

    first_state(1)
    start_edges(1, 0)

    @pl.when(north)
    def _():
        beside_copy(0).start()

    @pl.when(south)
    def _():
        beside_copy(1).start()

    @pl.when(band == 0)
    def _():
        rows_in[:, :, 0] = jnp.zeros((2, SUBSTEPS, OWN, 1, REGION), f32)

    @pl.when(band == 3)
    def _():
        rows_in[:, :, 1] = jnp.zeros((2, SUBSTEPS, OWN, 1, REGION), f32)

    own_class = classes[rows8, :]
    turned = jnp.zeros((ROWS, LON), f32)
    for level in range(CLASSES):
        turned = jnp.where(own_class == level, refraction[level, freq], turned)
    store_wrapped(turning, turned)

    for offset in range(3):
        there = jnp.minimum(jnp.maximum(band + offset - 1, 0), 3)
        for col in range(LON // LANES):
            masks[offset, col] = sea[
                pl.ds(pl.multiple_of(there * ROWS, ROWS), ROWS), col * LANES : (col + 1) * LANES
            ].astype(f32)

    def store_split(part, rows, value):
        high = value.astype(bf16)
        split[part, rows, :] = high
        split[2 + part, rows, :] = (value - high.astype(f32)).astype(bf16)

    load_interp.wait()

    @pl.loop(0, COMPS // LANES)
    def _(b):
        span = pl.ds(pl.multiple_of(b * LANES, LANES), LANES)
        store_split(0, span, interp[span, :])
        store_split(1, span, interp[:, span].T)

    wait_bytes(gathered, cur_recv)

    lane = lax.broadcasted_iota(jnp.int32, (ROWS, LANES), 1)
    left = lane < 64
    for u in range(TILES // 2):
        one = gathered[inverse[2 * u]]
        two = gathered[inverse[2 * u + 1]]
        east_part = 0.025 * jnp.where(left, one, pltpu.roll(two, 64, 1))
        north_part = 0.025 * jnp.where(left, pltpu.roll(one, 64, 1), two)
        for place in (u + 1,) + ((0,) if u == TILES // 2 - 1 else ()) + ((TILES // 2 + 1,) if u == 0 else ()):
            at = slice(place * LANES, (place + 1) * LANES)
            base_u[:, at] = east_part
            base_v[:, at] = north_part

    row = lax.broadcasted_iota(jnp.int32, (ROWS, PIECE), 0)
    speed = courant[freq]

    def advanced(half, step, i, piece):
        lo = piece * PIECE
        at = slice(lo, lo + PIECE)
        fixed = slice(half * HALF + lo, half * HALF + lo + PIECE)
        centre = state[half, step, i + 1, :, at]
        west_lo = lo - LANES if lo else REGION - LANES
        east_lo = (lo + PIECE) % REGION
        west_piece = state[half, step, i + 1, :, west_lo : west_lo + LANES]
        east_piece = state[half, step, i + 1, :, east_lo : east_lo + LANES]
        wide = jnp.concatenate([west_piece, centre, east_piece], axis=1)
        west = pltpu.roll(wide, 1, 1)[:, LANES:-LANES]
        east = pltpu.roll(wide, PIECE + 2 * LANES - 1, 1)[:, LANES:-LANES]
        below = jnp.where(row == 0, rows_in[half, step, 0, i, :, at], pltpu.roll(centre, 1, 0))
        above = jnp.where(row == ROWS - 1, rows_in[half, step, 1, i, :, at], pltpu.roll(centre, ROWS - 1, 0))
        before = state[half, step, i, :, at]
        after = state[half, step, i + 2, :, at]
        cos_d = cosine[first_dir + i]
        ax = base_u[:, fixed] + speed * cos_d
        ay = base_v[:, fixed] + speed * sine[first_dir + i]
        turn = turning[:, fixed] * cos_d
        change = (
            jnp.maximum(ax, 0.0) * (centre - west) + jnp.minimum(ax, 0.0) * (east - centre)
            + (jnp.maximum(ay, 0.0) * (centre - below) + jnp.minimum(ay, 0.0) * (above - centre))
            + (jnp.maximum(turn, 0.0) * (centre - before) + jnp.minimum(turn, 0.0) * (after - centre))
        )
        return ocean[:, fixed] * (centre - change)

    def propagate(half):
        for step in range(SUBSTEPS - 1):
            finish_edges(half, step)

            @pl.loop(0, OWN)
            def _(i):
                for piece in range(REGION // PIECE):
                    at = slice(piece * PIECE, (piece + 1) * PIECE)
                    new = advanced(half, step, i, piece)
                    state[half, step + 1, i + 1, :, at] = new
                    rows_out[half, step + 1, 0, i, :, at] = new[ROWS - 1 :, :]
                    rows_out[half, step + 1, 1, i, :, at] = new[:1, :]

            start_edges(half, step + 1)

        finish_edges(half, SUBSTEPS - 1)

        @pl.loop(0, OWN)
        def _(i):
            for piece in range(REGION // PIECE):
                new = advanced(half, SUBSTEPS - 1, i, piece)
                for tile in range(PIECE // LANES):
                    place = piece * (PIECE // LANES) + tile
                    if 1 <= place <= HALF // LANES:
                        col = half * (HALF // LANES) + place - 1
                        first = (col // 4) * ROWS * BLOCK + col % 4
                        send1[pl.ds(first + i * 4, ROWS, stride=BLOCK), :] = new[:, tile * LANES : (tile + 1) * LANES]

        @pl.loop(0, TILES // 2)
        def _(k):
            spot = (low + k) % 4
            to = (
                ((plane + plane_offset(k // 4)) % PLANE) * PLANE + (spot // 2) * 4 + half * 2 + spot % 2
            )

            @pl.when(to != me)
            def _():
                pltpu.make_async_remote_copy(
                    src_ref=block_of(send1, order_of(to)),
                    dst_ref=block_of(recv1, me),
                    send_sem=in_send,
                    recv_sem=in_recv,
                    device_id={"comp": to},
                    device_id_type=MESH,
                ).start()

            @pl.when(to == me)
            def _():
                pltpu.make_async_copy(block_of(send1, order_of(to)), block_of(recv1, me), in_recv).start()

    propagate(0)
    propagate(1)
    wait_bytes(recv1, in_recv)

    @pl.loop(0, COMPS // CHUNK)
    def _(c):
        rows = pl.ds(pl.multiple_of(c * CHUNK, 16), CHUNK)
        for q in range(4):
            value = recv1[pl.ds(c * (CHUNK * 4) + q, CHUNK, stride=4), :]
            at = slice(q * LANES, (q + 1) * LANES)
            high = value.astype(bf16)
            points[rows, at] = value
            points_hi[rows, at] = high
            points_lo[rows, at] = (value - high.astype(f32)).astype(bf16)

    my_group = my_order // PLANE

    def source_chunk(c, drift):
        group = (plane + plane_offset(c)) % PLANE
        rows = pl.ds(pl.multiple_of(group * CHUNK, 16), CHUNK)
        matrix = jnp.concatenate([split[part, rows, :] for part in range(4)], axis=0)
        both = jnp.dot(matrix, points_hi[...], preferred_element_type=f32)
        more = jnp.dot(matrix[: 2 * CHUNK], points_lo[...], preferred_element_type=f32)
        sums = both[: 2 * CHUNK] + (both[2 * CHUNK :] + more)
        forward, backward = sums[:CHUNK], sums[CHUNK:]
        wave = points[rows, :]
        new = wave + 0.5 * (forward * backward - 0.5 * wave * (forward + backward))
        for q in range(4):
            send2[pl.ds(group * (CHUNK * 4) + q, CHUNK, stride=4), :] = new[:, q * LANES : (q + 1) * LANES]

        @pl.loop(0, PLANE)
        def _(e):
            to = group * PLANE + (low + e) % PLANE

            @pl.when(to != me)
            def _():
                pltpu.make_async_remote_copy(
                    src_ref=block_of(send2, to),
                    dst_ref=block_of(recv2, my_order),
                    send_sem=out_send,
                    recv_sem=out_recv.at[my_group],
                    device_id={"comp": to},
                    device_id_type=MESH,
                ).start()

            @pl.when(to == me)
            def _():
                pltpu.make_async_copy(
                    block_of(send2, me), block_of(recv2, my_order), out_recv.at[my_group]
                ).start()

        held = weights[rows, :]
        return tuple(
            drift[a] + jnp.sum((held[:, a : a + 1] * new).reshape(CHUNK // 8, 8, POINTS), axis=0) for a in range(2)
        )

    drift = lax.fori_loop(
        0, PLANE, source_chunk, (jnp.zeros((8, POINTS), f32), jnp.zeros((8, POINTS), f32))
    )
    for a in range(2):
        total = jnp.sum(drift[a], axis=0, keepdims=True)
        for q in range(4):
            drift_block[a * 4 + q : a * 4 + q + 1, :] = total[:, q * LANES : (q + 1) * LANES]

    my_drift = drift_all.at[my_order]

    @pl.loop(1, TILES)
    def _(t):
        pltpu.make_async_remote_copy(
            src_ref=drift_block,
            dst_ref=my_drift,
            send_sem=drift_send,
            recv_sem=drift_recv,
            device_id={"comp": (me + t) % TILES},
            device_id_type=MESH,
        ).start()

    pltpu.make_async_copy(drift_block, my_drift, drift_recv).start()

    wait_bytes(gathered.at[: TILES - 1], cur_send)
    wait_bytes(recv1.at[: (TILES - 1) * BLOCK], in_send)

    @pl.when(north)
    def _():
        beside_copy(0).wait_send()
        beside_copy(1).wait_recv()

    @pl.when(south)
    def _():
        beside_copy(1).wait_send()
        beside_copy(0).wait_recv()

    @pl.loop(0, PLANE)
    def _(g):
        group_rows = pl.ds(pl.multiple_of(g * PLANE * BLOCK, 8), PLANE * BLOCK)
        wait_bytes(recv2.at[group_rows], out_recv.at[g])

        @pl.loop(0, OWN)
        def _(i):
            for q in range(4):
                cols = pl.ds(pl.multiple_of(g * 4 * LANES + q * LANES, LANES), LANES)
                out[i, :, cols] = recv2[pl.ds(g * PLANE * BLOCK + q + i * 4, ROWS, stride=BLOCK), :]

        cols = pl.ds(pl.multiple_of(g * 4 * LANES, LANES), 4 * LANES)
        pltpu.make_async_copy(out.at[:, :, cols], out_any.at[:, :, cols], store_sem).start()

    wait_bytes(drift_all, drift_recv)
    tile = owner[me]
    row1 = lax.broadcasted_iota(jnp.int32, (ROWS, LANES), 0)

    def twice(value, half):
        other = pltpu.roll(value, 64, 1)
        return jnp.where(half == 0, value, other), jnp.where(half == 0, other, value)

    def mask(which_tile, offset):
        at_left, at_right = twice(masks[offset + 1, which_tile // 2], which_tile % 2)
        return jnp.where(left, at_left, at_right)

    own = mask(tile, 0)
    held = cat[...] * own
    west_tile, east_tile = (tile + TILES - 1) % TILES, (tile + 1) % TILES
    held_w = gathered[inverse[west_tile]] * mask(west_tile, 0)
    held_e = gathered[inverse[east_tile]] * mask(east_tile, 0)
    held_s = jnp.where(south, beside[0] * mask(tile, -1), 0.0)
    held_n = jnp.where(north, beside[1] * mask(tile, 1), 0.0)
    west = jnp.where(lane % 64 == 0, pltpu.roll(held_w, 65, 1), pltpu.roll(held, 1, 1))
    east = jnp.where(lane % 64 == 63, pltpu.roll(held_e, 63, 1), pltpu.roll(held, 127, 1))
    below = jnp.where(row1 == 0, pltpu.roll(held_s, 1, 0), pltpu.roll(held, 1, 0))
    above = jnp.where(row1 == ROWS - 1, pltpu.roll(held_n, 7, 0), pltpu.roll(held, 7, 0))
    lap = west + east + below + above - 4.0 * held
    quarter = (tile % 8) // 2
    sums = [jnp.zeros((ROWS, LANES), f32), jnp.zeros((ROWS, LANES), f32)]
    for r in range(ROWS):
        piece = drift_all[(tile // 8) * ROWS + r]
        for a in range(2):
            chosen = jnp.sum(jnp.where(row1 == quarter + 4 * a, piece, 0.0), axis=0, keepdims=True)
            sums[a] = jnp.where(row1 == r, chosen, sums[a])
    eastward, _ = twice(sums[0], tile % 2)
    _, northward = twice(sums[1], tile % 2)
    stokes = jnp.where(left, eastward, northward)
    turn = jnp.where(left, 1.0, -1.0) * coriolis[rows8, :]
    other = pltpu.roll(held + stokes, 64, 1)
    result = own * (held + 0.5 * (turn * other + 0.2 * lap - 0.1 * held))
    ocean_out[0] = result[:, :64]
    ocean_out[1] = result[:, 64:]

    wait_bytes(drift_all.at[: TILES - 1], drift_send)
    wait_bytes(recv2.at[: (TILES - 1) * BLOCK], out_send)
    wait_bytes(out, store_sem)


def tables():
    angles = np.arange(DIRS, dtype=np.float32) * np.float32(2.0 * math.pi / DIRS)
    cosine, sine = np.cos(angles).astype(np.float32), np.sin(angles).astype(np.float32)
    k = np.arange(COMPS)
    scale = (np.float32(0.2) * (k // DIRS + 1).astype(np.float32) / np.float32(FREQ)).astype(np.float32)
    weights = np.stack([scale * cosine[k % DIRS], scale * sine[k % DIRS]], axis=1)
    latitude = -1.2 + 2.4 * (np.arange(TOTAL_ROWS, dtype=np.float32) + np.float32(0.5)) / TOTAL_ROWS
    coriolis = np.broadcast_to(np.sin(latitude.astype(np.float32))[:, None], (TOTAL_ROWS, LANES))
    return cosine, sine, weights.astype(np.float32), coriolis.astype(np.float32)


def local(spectrum, currents, group_courant, refraction, interp, sea_mask, depth_class, owner_map):
    cosine, sine, weights, coriolis = tables()
    index = jnp.arange(TILES, dtype=jnp.int32)
    inverse = jnp.sum(jnp.where(owner_map[None, :] == index[:, None], index[None, :], 0), axis=1)
    vmem, smem = pl.BlockSpec(memory_space=pltpu.VMEM), pl.BlockSpec(memory_space=pltpu.SMEM)
    anywhere = pl.BlockSpec(memory_space=pl.ANY)
    dma = pltpu.SemaphoreType.DMA
    extended = pltpu.VMEM((ROWS, LON + 2 * LANES), f32)
    blocks = pltpu.VMEM((TILES * BLOCK, LANES), f32)
    edge_rows = pltpu.VMEM((2, SUBSTEPS, 2, OWN, 1, REGION), f32)
    return pl.pallas_call(
        wave_kernel,
        out_shape=(
            jax.ShapeDtypeStruct((OWN, ROWS, LON), f32),
            jax.ShapeDtypeStruct((2, ROWS, LON // TILES), f32),
        ),
        in_specs=[vmem, vmem, vmem, vmem, anywhere, vmem, vmem] + [smem] * 6,
        out_specs=(anywhere, vmem),
        scratch_shapes=[
            pltpu.VMEM((2, SUBSTEPS, OWN + 2, ROWS, REGION), f32),
            edge_rows,
            edge_rows,
            extended,
            extended,
            extended,
            extended,
            blocks,
            blocks,
            blocks,
            blocks,
            pltpu.VMEM((OWN, ROWS, LON), f32),
            pltpu.VMEM((COMPS, COMPS), f32),
            pltpu.VMEM((4, COMPS, COMPS), bf16),
            pltpu.VMEM((COMPS, POINTS), f32),
            pltpu.VMEM((COMPS, POINTS), bf16),
            pltpu.VMEM((COMPS, POINTS), bf16),
            pltpu.VMEM((ROWS, LANES), f32),
            pltpu.VMEM((TILES, ROWS, LANES), f32),
            pltpu.VMEM((2, ROWS, LANES), f32),
            pltpu.VMEM((8, LANES), f32),
            pltpu.VMEM((TILES, 8, LANES), f32),
            pltpu.VMEM((3, LON // LANES, ROWS, LANES), f32),
            dma,
            dma,
            dma,
            dma((2,)),
            dma((2,)),
            dma((2, SUBSTEPS, 4)),
            dma((2, SUBSTEPS, 4)),
            dma,
            dma,
            dma,
            dma((PLANE,)),
            dma,
            dma,
            dma,
        ],
        compiler_params=pltpu.CompilerParams(
            collective_id=0, has_side_effects=True, vmem_limit_bytes=62 * 2**20
        ),
        name="waves",
    )(
        spectrum, currents, sea_mask, depth_class, interp, jnp.asarray(weights), jnp.asarray(coriolis), group_courant,
        refraction, owner_map, inverse, jnp.asarray(cosine), jnp.asarray(sine),
    )


def solution(mesh):
    in_specs = (P("comp", "band", None), P(None, "band", "comp"), P(), P(), P(), P(), P(), P())
    out_specs = (P("comp", "band", None), P(None, "band", "comp"))
    return jax.shard_map(local, mesh=mesh, in_specs=in_specs, out_specs=out_specs, check_vma=False)
```

```python
import math

import jax
import jax.numpy as jnp
import numpy as np
from jax import lax
from jax.experimental import pallas as pl
from jax.experimental.pallas import tpu as pltpu
from jax.sharding import PartitionSpec as P

DIRS = 36
FREQ = 32
CLASSES = 8
SUBSTEPS = 4
COMPS = 1152
OWN = 18
ROWS = 8
TOTAL_ROWS = 32
LON = 4096
TILES = 64
PLANE = 8
LANES = 128
BLOCK = OWN * 4
CHUNK = 144
POINTS = 512
PIECE = 1024
HALF = 2048
HALO = 4
WIDE = OWN + 2 * HALO
PAIRS = ((4, 0), (3, 7), (5, 1), (2, 6))
INNER = (4, 14)
MESH = pl.DeviceIdType.MESH
f32 = jnp.float32
bf16 = jnp.bfloat16


def plane_offset(step):
    return 4 + (1 - 2 * (step % 2)) * ((step + 1) // 2)


def block_of(ref, which):
    return ref.at[pl.ds(pl.multiple_of(which * BLOCK, 8), BLOCK)]


def wait_bytes(ref, sem):
    pltpu.make_async_copy(ref, ref, sem).wait()


def wave_kernel(
    spectrum_any, currents, sea, classes, interp_any, weights, coriolis, courant, refraction, owner, inverse, cosine, sine,
    out_any, ocean_out,
    state, rows_out, rows_in, base_u, base_v, turning, ocean, send1, recv1, send2, recv2, out, interp, split,
    points, points_hi, points_lo, cat, gathered, beside, drift_block, drift_all, masks,
    interp_sem, spec_sem, cur_send, cur_recv, beside_send, beside_recv, row_send, row_recv, dir_send, dir_recv,
    in_send, in_recv, out_send, out_recv, drift_send, drift_recv, store_sem,
):
    me = lax.axis_index("comp")
    band = lax.axis_index("band")
    plane = me // PLANE
    low = me % PLANE
    partner = me + 1 - 2 * (me % 2)
    freq = me // 2
    first_dir = (me % 2) * OWN
    south = band > 0
    north = band < 3

    load_interp = pltpu.make_async_copy(interp_any, interp, interp_sem)
    load_interp.start()
    load_spectrum = pltpu.make_async_copy(spectrum_any, state.at[0, HALO : HALO + OWN], spec_sem)
    load_spectrum.start()

    barrier = pltpu.get_barrier_semaphore()

    @pl.loop(1, TILES)
    def _(t):
        pl.semaphore_signal(barrier, inc=1, device_id={"comp": (me + t) % TILES}, device_id_type=MESH)

    @pl.when(south)
    def _():
        pl.semaphore_signal(barrier, inc=1, device_id={"band": band - 1}, device_id_type=MESH)

    @pl.when(north)
    def _():
        pl.semaphore_signal(barrier, inc=1, device_id={"band": band + 1}, device_id_type=MESH)

    rows8 = pl.ds(pl.multiple_of(band * ROWS, ROWS), ROWS)

    ocean[...] = sea[rows8, :].astype(f32)
    cat[:, :64] = currents[0]
    cat[:, 64:] = currents[1]

    def span(step, part):
        return ((5 + step, 21 - step), (1 + step, 5 + step), (21 - step, 25 - step))[part]

    def row_copy(step, part, half, side):
        lo, hi = span(step, part)
        cols = slice(half * HALF, (half + 1) * HALF)
        return pltpu.make_async_remote_copy(
            src_ref=rows_out.at[step, side, lo:hi, :, cols],
            dst_ref=rows_in.at[step, side, lo:hi, :, cols],
            send_sem=row_send.at[step, part, half, side],
            recv_sem=row_recv.at[step, part, half, side],
            device_id={"band": band + 1 - 2 * side},
            device_id_type=MESH,
        )

    def start_rows(step, parts, halves=(0, 1)):
        @pl.when(north)
        def _():
            for part in parts:
                for half in halves:
                    row_copy(step, part, half, 0).start()

        @pl.when(south)
        def _():
            for part in parts:
                for half in halves:
                    row_copy(step, part, half, 1).start()

    def finish_rows(step, parts, halves=(0, 1)):
        @pl.when(south)
        def _():
            for part in parts:
                for half in halves:
                    row_copy(step, part, half, 0).wait_recv()
                    row_copy(step, part, half, 1).wait_send()

        @pl.when(north)
        def _():
            for part in parts:
                for half in halves:
                    row_copy(step, part, half, 1).wait_recv()
                    row_copy(step, part, half, 0).wait_send()

    pieces = ((0, 2), (2, 3), (3, 4))

    def dir_copy(side, n):
        lo, hi = pieces[n]
        source = (OWN - HALO if side == 0 else 0) + lo
        to = (0 if side == 0 else HALO + OWN) + lo
        return pltpu.make_async_remote_copy(
            src_ref=spectrum_any.at[source : source + hi - lo],
            dst_ref=state.at[0, to : to + hi - lo],
            send_sem=dir_send.at[side, n],
            recv_sem=dir_recv.at[side, n],
            device_id={"comp": partner},
            device_id_type=MESH,
        )

    def start_dirs(n):
        dir_copy(0, n).start()
        dir_copy(1, n).start()

    def mask_first(lo, hi):
        @pl.loop(lo, hi)
        def _(e):
            masked = state[0, e] * ocean[...]
            state[0, e] = masked
            rows_out[0, 0, e] = masked[ROWS - 1 :, :]
            rows_out[0, 1, e] = masked[:1, :]

    load_spectrum.wait()
    mask_first(HALO, HALO + OWN)
    pl.semaphore_wait(barrier, TILES - 1 + jnp.where(south, 1, 0) + jnp.where(north, 1, 0))

    def cur_copy(t):
        return pltpu.make_async_remote_copy(
            src_ref=cat,
            dst_ref=gathered.at[me],
            send_sem=cur_send,
            recv_sem=cur_recv,
            device_id={"comp": (me + t) % TILES},
            device_id_type=MESH,
        )

    def beside_copy(side):
        return pltpu.make_async_remote_copy(
            src_ref=cat,
            dst_ref=beside.at[side],
            send_sem=beside_send.at[side],
            recv_sem=beside_recv.at[side],
            device_id={"band": band + 1 - 2 * side},
            device_id_type=MESH,
        )

    start_rows(0, (0,))

    @pl.loop(1, TILES)
    def _(t):
        cur_copy(t).start()

    pltpu.make_async_copy(cat, gathered.at[me], cur_recv).start()

    start_dirs(0)

    @pl.when(north)
    def _():
        beside_copy(0).start()

    @pl.when(south)
    def _():
        beside_copy(1).start()

    @pl.when(band == 0)
    def _():
        rows_in[:, 0] = jnp.zeros((SUBSTEPS, WIDE, 1, LON), f32)

    @pl.when(band == 3)
    def _():
        rows_in[:, 1] = jnp.zeros((SUBSTEPS, WIDE, 1, LON), f32)

    own_class = classes[rows8, :]
    turned = jnp.zeros((ROWS, LON), f32)
    for level in range(CLASSES):
        turned = jnp.where(own_class == level, refraction[level, freq], turned)
    turning[...] = turned

    for offset in range(3):
        there = jnp.minimum(jnp.maximum(band + offset - 1, 0), 3)
        for col in range(LON // LANES):
            masks[offset, col] = sea[
                pl.ds(pl.multiple_of(there * ROWS, ROWS), ROWS), col * LANES : (col + 1) * LANES
            ].astype(f32)

    def store_split(part, rows, value):
        high = value.astype(bf16)
        split[part, rows, :] = high
        split[2 + part, rows, :] = (value - high.astype(f32)).astype(bf16)

    load_interp.wait()

    @pl.loop(0, COMPS // LANES)
    def _(b):
        span = pl.ds(pl.multiple_of(b * LANES, LANES), LANES)
        store_split(0, span, interp[span, :])
        store_split(1, span, interp[:, span].T)

    wait_bytes(gathered, cur_recv)

    lane = lax.broadcasted_iota(jnp.int32, (ROWS, LANES), 1)
    left = lane < 64
    for u in range(TILES // 2):
        one = gathered[inverse[2 * u]]
        two = gathered[inverse[2 * u + 1]]
        east_part = 0.025 * jnp.where(left, one, pltpu.roll(two, 64, 1))
        north_part = 0.025 * jnp.where(left, pltpu.roll(one, 64, 1), two)
        at = slice(u * LANES, (u + 1) * LANES)
        base_u[:, at] = east_part
        base_v[:, at] = north_part

    row = lax.broadcasted_iota(jnp.int32, (ROWS, PIECE), 0)
    speed = courant[freq]

    def advanced(step, e, piece):
        lo = piece * PIECE
        at = slice(lo, lo + PIECE)
        centre = state[step, e, :, at]
        west_lo, east_lo = (lo - LANES) % LON, (lo + PIECE) % LON
        west_piece = state[step, e, :, west_lo : west_lo + LANES]
        east_piece = state[step, e, :, east_lo : east_lo + LANES]
        wide = jnp.concatenate([west_piece, centre, east_piece], axis=1)
        west = pltpu.roll(wide, 1, 1)[:, LANES:-LANES]
        east = pltpu.roll(wide, PIECE + 2 * LANES - 1, 1)[:, LANES:-LANES]
        below = jnp.where(row == 0, rows_in[step, 0, e, :, at], pltpu.roll(centre, 1, 0))
        above = jnp.where(row == ROWS - 1, rows_in[step, 1, e, :, at], pltpu.roll(centre, ROWS - 1, 0))
        before = state[step, e - 1, :, at]
        after = state[step, e + 1, :, at]
        direction = (first_dir + e + DIRS - HALO) % DIRS
        cos_d = cosine[direction]
        ax = base_u[:, at] + speed * cos_d
        ay = base_v[:, at] + speed * sine[direction]
        turn = turning[:, at] * cos_d
        change = (
            jnp.maximum(ax, 0.0) * (centre - west) + jnp.minimum(ax, 0.0) * (east - centre)
            + (jnp.maximum(ay, 0.0) * (centre - below) + jnp.minimum(ay, 0.0) * (above - centre))
            + (jnp.maximum(turn, 0.0) * (centre - before) + jnp.minimum(turn, 0.0) * (after - centre))
        )
        return ocean[:, at] * (centre - change)

    def middle(step, part, halves=(0, 1)):
        lo, hi = span(step, part)

        @pl.loop(lo, hi)
        def _(e):
            for piece in range(halves[0] * 2, halves[-1] * 2 + 2):
                at = slice(piece * PIECE, (piece + 1) * PIECE)
                new = advanced(step, e, piece)
                state[step + 1, e, :, at] = new
                rows_out[step + 1, 0, e, :, at] = new[ROWS - 1 :, :]
                rows_out[step + 1, 1, e, :, at] = new[:1, :]

    def last(part, halves=(0, 1)):
        lo, hi = span(SUBSTEPS - 1, part)

        @pl.loop(lo, hi)
        def _(e):
            for piece in range(halves[0] * 2, halves[-1] * 2 + 2):
                new = advanced(SUBSTEPS - 1, e, piece)
                for tile in range(PIECE // LANES):
                    col = piece * (PIECE // LANES) + tile
                    first = (col // 4) * ROWS * BLOCK + col % 4
                    send1[pl.ds(first + (e - HALO) * 4, ROWS, stride=BLOCK), :] = (
                        new[:, tile * LANES : (tile + 1) * LANES]
                    )

    def send_blocks(group, lo, hi):
        @pl.loop(0, 16)
        def _(k):
            away = jnp.where(k < 8, PAIRS[group][0], PAIRS[group][1])
            to = ((plane + away) % PLANE) * PLANE + (low + k) % PLANE
            source = send1.at[pl.ds(pl.multiple_of(to * BLOCK + lo * 4, 8), (hi - lo) * 4)]
            target = recv1.at[pl.ds(pl.multiple_of(me * BLOCK + lo * 4, 8), (hi - lo) * 4)]

            @pl.when(to != me)
            def _():
                pltpu.make_async_remote_copy(
                    src_ref=source,
                    dst_ref=target,
                    send_sem=in_send,
                    recv_sem=in_recv,
                    device_id={"comp": to},
                    device_id_type=MESH,
                ).start()

            @pl.when(to == me)
            def _():
                pltpu.make_async_copy(source, target, in_recv).start()

    inner, sides = (0,), (1, 2)
    for step in range(SUBSTEPS - 1):
        for half in range(2):
            finish_rows(step, inner, (half,))
            middle(step, 0, (half,))
            start_rows(step + 1, inner, (half,))
        if step < 2:
            start_dirs(step + 1)
    for half in range(2):
        finish_rows(SUBSTEPS - 1, inner, (half,))
        last(0, (half,))
    for side in range(2):
        for n in range(3):
            dir_copy(side, n).wait()
    mask_first(0, HALO)
    mask_first(HALO + OWN, WIDE)
    start_rows(0, sides)
    send_blocks(0, *INNER)
    for step in range(SUBSTEPS - 1):
        finish_rows(step, sides)
        middle(step, 1)
        middle(step, 2)
        start_rows(step + 1, sides)
        send_blocks(step + 1, *INNER)
    finish_rows(SUBSTEPS - 1, sides)
    last(1)
    last(2)
    for group in range(4):
        send_blocks(group, 0, HALO)
        send_blocks(group, OWN - HALO, OWN)
    wait_bytes(recv1, in_recv)

    @pl.loop(0, COMPS // CHUNK)
    def _(c):
        rows = pl.ds(pl.multiple_of(c * CHUNK, 16), CHUNK)
        for q in range(4):
            value = recv1[pl.ds(c * (CHUNK * 4) + q, CHUNK, stride=4), :]
            at = slice(q * LANES, (q + 1) * LANES)
            high = value.astype(bf16)
            points[rows, at] = value
            points_hi[rows, at] = high
            points_lo[rows, at] = (value - high.astype(f32)).astype(bf16)

    my_group = me // PLANE

    def source_chunk(c, drift):
        group = (plane + plane_offset(c)) % PLANE
        rows = pl.ds(pl.multiple_of(group * CHUNK, 16), CHUNK)
        matrix = jnp.concatenate([split[part, rows, :] for part in range(4)], axis=0)
        both = jnp.dot(matrix, points_hi[...], preferred_element_type=f32)
        more = jnp.dot(matrix[: 2 * CHUNK], points_lo[...], preferred_element_type=f32)
        sums = both[: 2 * CHUNK] + (both[2 * CHUNK :] + more)
        forward, backward = sums[:CHUNK], sums[CHUNK:]
        wave = points[rows, :]
        new = wave + 0.5 * (forward * backward - 0.5 * wave * (forward + backward))
        for q in range(4):
            send2[pl.ds(group * (CHUNK * 4) + q, CHUNK, stride=4), :] = new[:, q * LANES : (q + 1) * LANES]

        @pl.loop(0, PLANE)
        def _(e):
            to = group * PLANE + (low + e) % PLANE

            @pl.when(to != me)
            def _():
                pltpu.make_async_remote_copy(
                    src_ref=block_of(send2, to),
                    dst_ref=block_of(recv2, me),
                    send_sem=out_send,
                    recv_sem=out_recv.at[my_group],
                    device_id={"comp": to},
                    device_id_type=MESH,
                ).start()

            @pl.when(to == me)
            def _():
                pltpu.make_async_copy(
                    block_of(send2, me), block_of(recv2, me), out_recv.at[my_group]
                ).start()

        held = weights[rows, :]
        return tuple(
            drift[a] + jnp.sum((held[:, a : a + 1] * new).reshape(CHUNK // 8, 8, POINTS), axis=0) for a in range(2)
        )

    drift = lax.fori_loop(
        0, PLANE, source_chunk, (jnp.zeros((8, POINTS), f32), jnp.zeros((8, POINTS), f32))
    )
    for a in range(2):
        total = jnp.sum(drift[a], axis=0, keepdims=True)
        for q in range(4):
            drift_block[a * 4 + q : a * 4 + q + 1, :] = total[:, q * LANES : (q + 1) * LANES]

    my_drift = drift_all.at[me]

    @pl.loop(1, TILES)
    def _(t):
        pltpu.make_async_remote_copy(
            src_ref=drift_block,
            dst_ref=my_drift,
            send_sem=drift_send,
            recv_sem=drift_recv,
            device_id={"comp": (me + t) % TILES},
            device_id_type=MESH,
        ).start()

    pltpu.make_async_copy(drift_block, my_drift, drift_recv).start()

    wait_bytes(gathered.at[: TILES - 1], cur_send)
    wait_bytes(recv1.at[: (TILES - 1) * BLOCK], in_send)

    @pl.when(north)
    def _():
        beside_copy(0).wait_send()
        beside_copy(1).wait_recv()

    @pl.when(south)
    def _():
        beside_copy(1).wait_send()
        beside_copy(0).wait_recv()

    @pl.loop(0, PLANE)
    def _(n):
        g = (plane + PLANE - plane_offset(n)) % PLANE
        group_rows = pl.ds(pl.multiple_of(g * PLANE * BLOCK, 8), PLANE * BLOCK)
        wait_bytes(recv2.at[group_rows], out_recv.at[g])

        @pl.loop(0, OWN)
        def _(i):
            for q in range(4):
                cols = pl.ds(pl.multiple_of(g * 4 * LANES + q * LANES, LANES), LANES)
                out[i, :, cols] = recv2[pl.ds(g * PLANE * BLOCK + q + i * 4, ROWS, stride=BLOCK), :]

        cols = pl.ds(pl.multiple_of(g * 4 * LANES, LANES), 4 * LANES)
        pltpu.make_async_copy(out.at[:, :, cols], out_any.at[:, :, cols], store_sem).start()

    wait_bytes(drift_all, drift_recv)
    tile = owner[me]
    row1 = lax.broadcasted_iota(jnp.int32, (ROWS, LANES), 0)

    def twice(value, half):
        other = pltpu.roll(value, 64, 1)
        return jnp.where(half == 0, value, other), jnp.where(half == 0, other, value)

    def mask(which_tile, offset):
        at_left, at_right = twice(masks[offset + 1, which_tile // 2], which_tile % 2)
        return jnp.where(left, at_left, at_right)

    own = mask(tile, 0)
    held = cat[...] * own
    west_tile, east_tile = (tile + TILES - 1) % TILES, (tile + 1) % TILES
    held_w = gathered[inverse[west_tile]] * mask(west_tile, 0)
    held_e = gathered[inverse[east_tile]] * mask(east_tile, 0)
    held_s = jnp.where(south, beside[0] * mask(tile, -1), 0.0)
    held_n = jnp.where(north, beside[1] * mask(tile, 1), 0.0)
    west = jnp.where(lane % 64 == 0, pltpu.roll(held_w, 65, 1), pltpu.roll(held, 1, 1))
    east = jnp.where(lane % 64 == 63, pltpu.roll(held_e, 63, 1), pltpu.roll(held, 127, 1))
    below = jnp.where(row1 == 0, pltpu.roll(held_s, 1, 0), pltpu.roll(held, 1, 0))
    above = jnp.where(row1 == ROWS - 1, pltpu.roll(held_n, 7, 0), pltpu.roll(held, 7, 0))
    lap = west + east + below + above - 4.0 * held
    quarter = (tile % 8) // 2
    sums = [jnp.zeros((ROWS, LANES), f32), jnp.zeros((ROWS, LANES), f32)]
    for r in range(ROWS):
        piece = drift_all[(tile // 8) * ROWS + r]
        for a in range(2):
            chosen = jnp.sum(jnp.where(row1 == quarter + 4 * a, piece, 0.0), axis=0, keepdims=True)
            sums[a] = jnp.where(row1 == r, chosen, sums[a])
    eastward, _ = twice(sums[0], tile % 2)
    _, northward = twice(sums[1], tile % 2)
    stokes = jnp.where(left, eastward, northward)
    turn = jnp.where(left, 1.0, -1.0) * coriolis[rows8, :]
    other = pltpu.roll(held + stokes, 64, 1)
    result = own * (held + 0.5 * (turn * other + 0.2 * lap - 0.1 * held))
    ocean_out[0] = result[:, :64]
    ocean_out[1] = result[:, 64:]

    wait_bytes(drift_all.at[: TILES - 1], drift_send)
    wait_bytes(recv2.at[: (TILES - 1) * BLOCK], out_send)
    wait_bytes(out, store_sem)


def tables():
    angles = np.arange(DIRS, dtype=np.float32) * np.float32(2.0 * math.pi / DIRS)
    cosine, sine = np.cos(angles).astype(np.float32), np.sin(angles).astype(np.float32)
    k = np.arange(COMPS)
    scale = (np.float32(0.2) * (k // DIRS + 1).astype(np.float32) / np.float32(FREQ)).astype(np.float32)
    weights = np.stack([scale * cosine[k % DIRS], scale * sine[k % DIRS]], axis=1)
    latitude = -1.2 + 2.4 * (np.arange(TOTAL_ROWS, dtype=np.float32) + np.float32(0.5)) / TOTAL_ROWS
    coriolis = np.broadcast_to(np.sin(latitude.astype(np.float32))[:, None], (TOTAL_ROWS, LANES))
    return cosine, sine, weights.astype(np.float32), coriolis.astype(np.float32)


def local(spectrum, currents, group_courant, refraction, interp, sea_mask, depth_class, owner_map):
    cosine, sine, weights, coriolis = tables()
    index = jnp.arange(TILES, dtype=jnp.int32)
    inverse = jnp.sum(jnp.where(owner_map[None, :] == index[:, None], index[None, :], 0), axis=1)
    vmem, smem = pl.BlockSpec(memory_space=pltpu.VMEM), pl.BlockSpec(memory_space=pltpu.SMEM)
    anywhere = pl.BlockSpec(memory_space=pl.ANY)
    dma = pltpu.SemaphoreType.DMA
    field = pltpu.VMEM((ROWS, LON), f32)
    blocks = pltpu.VMEM((TILES * BLOCK, LANES), f32)
    edge_rows = pltpu.VMEM((SUBSTEPS, 2, WIDE, 1, LON), f32)
    return pl.pallas_call(
        wave_kernel,
        out_shape=(
            jax.ShapeDtypeStruct((OWN, ROWS, LON), f32),
            jax.ShapeDtypeStruct((2, ROWS, LON // TILES), f32),
        ),
        in_specs=[anywhere, vmem, vmem, vmem, anywhere, vmem, vmem] + [smem] * 6,
        out_specs=(anywhere, vmem),
        scratch_shapes=[
            pltpu.VMEM((SUBSTEPS, WIDE, ROWS, LON), f32),
            edge_rows,
            edge_rows,
            field,
            field,
            field,
            field,
            blocks,
            blocks,
            blocks,
            blocks,
            pltpu.VMEM((OWN, ROWS, LON), f32),
            pltpu.VMEM((COMPS, COMPS), f32),
            pltpu.VMEM((4, COMPS, COMPS), bf16),
            pltpu.VMEM((COMPS, POINTS), f32),
            pltpu.VMEM((COMPS, POINTS), bf16),
            pltpu.VMEM((COMPS, POINTS), bf16),
            pltpu.VMEM((ROWS, LANES), f32),
            pltpu.VMEM((TILES, ROWS, LANES), f32),
            pltpu.VMEM((2, ROWS, LANES), f32),
            pltpu.VMEM((8, LANES), f32),
            pltpu.VMEM((TILES, 8, LANES), f32),
            pltpu.VMEM((3, LON // LANES, ROWS, LANES), f32),
            dma,
            dma,
            dma,
            dma,
            dma((2,)),
            dma((2,)),
            dma((SUBSTEPS, 3, 2, 2)),
            dma((SUBSTEPS, 3, 2, 2)),
            dma((2, 3)),
            dma((2, 3)),
            dma,
            dma,
            dma,
            dma((PLANE,)),
            dma,
            dma,
            dma,
        ],
        compiler_params=pltpu.CompilerParams(
            collective_id=0, has_side_effects=True, vmem_limit_bytes=62 * 2**20
        ),
        name="waves",
    )(
        spectrum, currents, sea_mask, depth_class, interp, jnp.asarray(weights), jnp.asarray(coriolis), group_courant,
        refraction, owner_map, inverse, jnp.asarray(cosine), jnp.asarray(sine),
    )


def solution(mesh):
    in_specs = (P("comp", "band", None), P(None, "band", "comp"), P(), P(), P(), P(), P(), P())
    out_specs = (P("comp", "band", None), P(None, "band", "comp"))
    return jax.shard_map(local, mesh=mesh, in_specs=in_specs, out_specs=out_specs, check_vma=False)
```

```python
import math

import jax
import jax.numpy as jnp
import numpy as np
from jax import lax
from jax.experimental import pallas as pl
from jax.experimental.pallas import tpu as pltpu
from jax.sharding import PartitionSpec as P

DIRS = 36
FREQ = 32
CLASSES = 8
SUBSTEPS = 4
COMPS = 1152
OWN = 18
ROWS = 8
TOTAL_ROWS = 32
LON = 4096
TILES = 64
PLANE = 8
LANES = 128
BLOCK = OWN * 4
CHUNK = 144
POINTS = 512
PIECE = 1024
HALF = 2048
HALO = 4
WIDE = OWN + 2 * HALO
PAIRS = ((4, 0), (3, 7), (5, 1), (2, 6))
INNER = (4, 14)
MESH = pl.DeviceIdType.MESH
f32 = jnp.float32
bf16 = jnp.bfloat16


def plane_offset(step):
    return 3 * (step + 1) % PLANE


def block_of(ref, which):
    return ref.at[pl.ds(pl.multiple_of(which * BLOCK, 8), BLOCK)]


def wait_bytes(ref, sem):
    pltpu.make_async_copy(ref, ref, sem).wait()


def wave_kernel(
    spectrum_any, currents, sea, classes, interp_any, weights, coriolis, courant, refraction, owner, inverse, cosine, sine,
    out_any, ocean_out,
    state, rows_out, rows_in, base_u, base_v, turning, ocean, send1, recv1, send2, recv2, out, interp, split,
    points, points_hi, points_lo, cat, gathered, beside, drift_block, drift_all, masks,
    interp_sem, spec_sem, cur_send, cur_recv, beside_send, beside_recv, row_send, row_recv, dir_send, dir_recv,
    in_send, in_recv, out_send, out_recv, drift_send, drift_recv, store_sem,
):
    me = lax.axis_index("comp")
    band = lax.axis_index("band")
    plane = me // PLANE
    low = me % PLANE
    partner = me + 1 - 2 * (me % 2)
    freq = me // 2
    first_dir = (me % 2) * OWN
    south = band > 0
    north = band < 3

    for n in range(0, OWN, 3):
        pltpu.make_async_copy(spectrum_any.at[n : n + 3], state.at[0, HALO + n : HALO + n + 3], spec_sem).start()

    barrier = pltpu.get_barrier_semaphore()

    @pl.loop(1, TILES)
    def _(t):
        pl.semaphore_signal(barrier, inc=1, device_id={"comp": (me + t) % TILES}, device_id_type=MESH)

    @pl.when(south)
    def _():
        pl.semaphore_signal(barrier, inc=1, device_id={"band": band - 1}, device_id_type=MESH)
        pl.semaphore_signal(barrier, inc=1, device_id={"comp": partner, "band": band - 1}, device_id_type=MESH)

    @pl.when(north)
    def _():
        pl.semaphore_signal(barrier, inc=1, device_id={"band": band + 1}, device_id_type=MESH)
        pl.semaphore_signal(barrier, inc=1, device_id={"comp": partner, "band": band + 1}, device_id_type=MESH)

    rows8 = pl.ds(pl.multiple_of(band * ROWS, ROWS), ROWS)

    ocean[...] = sea[rows8, :].astype(f32)
    cat[:, :64] = currents[0]
    cat[:, 64:] = currents[1]

    def span(step, part):
        return ((5 + step, 21 - step), (1 + step, 5 + step), (21 - step, 25 - step))[part]

    def row_copy(step, part, half, side):
        lo, hi = span(step, part) if step else (HALO, HALO + OWN)
        cols = slice(half * HALF, (half + 1) * HALF)
        return pltpu.make_async_remote_copy(
            src_ref=rows_out.at[step, side, lo:hi, :, cols],
            dst_ref=rows_in.at[step, side, lo:hi, :, cols],
            send_sem=row_send.at[step, part, half, side],
            recv_sem=row_recv.at[step, part, half, side],
            device_id={"band": band + 1 - 2 * side},
            device_id_type=MESH,
        )

    def start_rows(step, parts, halves=(0, 1)):
        @pl.when(north)
        def _():
            for part in parts:
                for half in halves:
                    row_copy(step, part, half, 0).start()

        @pl.when(south)
        def _():
            for part in parts:
                for half in halves:
                    row_copy(step, part, half, 1).start()

    def finish_rows(step, parts, halves=(0, 1)):
        @pl.when(south)
        def _():
            for part in parts:
                for half in halves:
                    row_copy(step, part, half, 0).wait_recv()
                    row_copy(step, part, half, 1).wait_send()

        @pl.when(north)
        def _():
            for part in parts:
                for half in halves:
                    row_copy(step, part, half, 1).wait_recv()
                    row_copy(step, part, half, 0).wait_send()

    def diagonal_copy(which, side):
        lo, to = ((19, 1), (4, 22))[which]
        return pltpu.make_async_remote_copy(
            src_ref=rows_out.at[0, side, lo : lo + 3],
            dst_ref=rows_in.at[0, side, to : to + 3],
            send_sem=row_send.at[0, 1 + which, 0, side],
            recv_sem=row_recv.at[0, 1 + which, 0, side],
            device_id={"comp": partner, "band": band + 1 - 2 * side},
            device_id_type=MESH,
        )

    pieces = ((0, 2), (2, 3), (3, 4))

    def dir_copy(side, n):
        lo, hi = pieces[n]
        source = (OWN - HALO if side == 0 else 0) + lo
        to = (0 if side == 0 else HALO + OWN) + lo
        return pltpu.make_async_remote_copy(
            src_ref=spectrum_any.at[source : source + hi - lo],
            dst_ref=state.at[0, to : to + hi - lo],
            send_sem=dir_send.at[side, n],
            recv_sem=dir_recv.at[side, n],
            device_id={"comp": partner},
            device_id_type=MESH,
        )

    def start_dirs(n):
        dir_copy(0, n).start()
        dir_copy(1, n).start()

    def mask_first(lo, hi):
        @pl.loop(lo, hi)
        def _(e):
            masked = state[0, e] * ocean[...]
            state[0, e] = masked
            if lo == HALO:
                rows_out[0, 0, e] = masked[ROWS - 1 :, :]
                rows_out[0, 1, e] = masked[:1, :]

    wait_bytes(state.at[0, HALO : HALO + OWN], spec_sem)
    mask_first(HALO, HALO + OWN)
    pl.semaphore_wait(barrier, TILES - 1 + jnp.where(south, 2, 0) + jnp.where(north, 2, 0))

    def cur_copy(t):
        return pltpu.make_async_remote_copy(
            src_ref=cat,
            dst_ref=gathered.at[me],
            send_sem=cur_send,
            recv_sem=cur_recv,
            device_id={"comp": (me + t) % TILES},
            device_id_type=MESH,
        )

    def beside_copy(side):
        return pltpu.make_async_remote_copy(
            src_ref=cat,
            dst_ref=beside.at[side],
            send_sem=beside_send.at[side],
            recv_sem=beside_recv.at[side],
            device_id={"band": band + 1 - 2 * side},
            device_id_type=MESH,
        )

    start_rows(0, (0,))

    @pl.loop(1, TILES)
    def _(t):
        cur_copy(t).start()

    pltpu.make_async_copy(cat, gathered.at[me], cur_recv).start()

    start_dirs(0)
    for n in range(0, COMPS, LANES):
        pltpu.make_async_copy(interp_any.at[n : n + LANES], interp.at[n : n + LANES], interp_sem).start()

    @pl.when(north)
    def _():
        beside_copy(0).start()
        diagonal_copy(0, 0).start()
        diagonal_copy(1, 0).start()

    @pl.when(south)
    def _():
        beside_copy(1).start()
        diagonal_copy(0, 1).start()
        diagonal_copy(1, 1).start()

    @pl.when(band == 0)
    def _():
        rows_in[:, 0] = jnp.zeros((SUBSTEPS, WIDE, 1, LON), f32)

    @pl.when(band == 3)
    def _():
        rows_in[:, 1] = jnp.zeros((SUBSTEPS, WIDE, 1, LON), f32)

    own_class = classes[rows8, :]
    turned = jnp.zeros((ROWS, LON), f32)
    for level in range(CLASSES):
        turned = jnp.where(own_class == level, refraction[level, freq], turned)
    turning[...] = turned

    for offset in range(3):
        there = jnp.minimum(jnp.maximum(band + offset - 1, 0), 3)
        for col in range(LON // LANES):
            masks[offset, col] = sea[
                pl.ds(pl.multiple_of(there * ROWS, ROWS), ROWS), col * LANES : (col + 1) * LANES
            ].astype(f32)

    def store_split(part, rows, value):
        high = value.astype(bf16)
        split[part, rows, :] = high
        split[2 + part, rows, :] = (value - high.astype(f32)).astype(bf16)

    wait_bytes(gathered, cur_recv)

    lane = lax.broadcasted_iota(jnp.int32, (ROWS, LANES), 1)
    left = lane < 64
    for u in range(TILES // 2):
        one = gathered[inverse[2 * u]]
        two = gathered[inverse[2 * u + 1]]
        east_part = 0.025 * jnp.where(left, one, pltpu.roll(two, 64, 1))
        north_part = 0.025 * jnp.where(left, pltpu.roll(one, 64, 1), two)
        at = slice(u * LANES, (u + 1) * LANES)
        base_u[:, at] = east_part
        base_v[:, at] = north_part

    row = lax.broadcasted_iota(jnp.int32, (ROWS, PIECE), 0)
    speed = courant[freq]

    def advanced(step, e, piece):
        lo = piece * PIECE
        at = slice(lo, lo + PIECE)
        centre = state[step, e, :, at]
        west_lo, east_lo = (lo - LANES) % LON, (lo + PIECE) % LON
        west_piece = state[step, e, :, west_lo : west_lo + LANES]
        east_piece = state[step, e, :, east_lo : east_lo + LANES]
        wide = jnp.concatenate([west_piece, centre, east_piece], axis=1)
        west = pltpu.roll(wide, 1, 1)[:, LANES:-LANES]
        east = pltpu.roll(wide, PIECE + 2 * LANES - 1, 1)[:, LANES:-LANES]
        below = jnp.where(row == 0, rows_in[step, 0, e, :, at], pltpu.roll(centre, 1, 0))
        above = jnp.where(row == ROWS - 1, rows_in[step, 1, e, :, at], pltpu.roll(centre, ROWS - 1, 0))
        before = state[step, e - 1, :, at]
        after = state[step, e + 1, :, at]
        direction = (first_dir + e + DIRS - HALO) % DIRS
        cos_d = cosine[direction]
        ax = base_u[:, at] + speed * cos_d
        ay = base_v[:, at] + speed * sine[direction]
        turn = turning[:, at] * cos_d
        change = (
            ax * jnp.where(ax > 0.0, centre - west, east - centre)
            + ay * jnp.where(ay > 0.0, centre - below, above - centre)
            + turn * jnp.where(turn > 0.0, centre - before, after - centre)
        )
        return ocean[:, at] * (centre - change)

    def middle(step, part, halves=(0, 1)):
        lo, hi = span(step, part)

        @pl.loop(lo, hi)
        def _(e):
            for piece in range(halves[0] * 2, halves[-1] * 2 + 2):
                at = slice(piece * PIECE, (piece + 1) * PIECE)
                new = advanced(step, e, piece)
                state[step + 1, e, :, at] = new
                rows_out[step + 1, 0, e, :, at] = new[ROWS - 1 :, :]
                rows_out[step + 1, 1, e, :, at] = new[:1, :]

    def last(part, halves=(0, 1)):
        lo, hi = span(SUBSTEPS - 1, part)

        @pl.loop(lo, hi)
        def _(e):
            for piece in range(halves[0] * 2, halves[-1] * 2 + 2):
                new = advanced(SUBSTEPS - 1, e, piece)
                for tile in range(PIECE // LANES):
                    col = piece * (PIECE // LANES) + tile
                    first = (col // 4) * ROWS * BLOCK + col % 4
                    send1[pl.ds(first + (e - HALO) * 4, ROWS, stride=BLOCK), :] = (
                        new[:, tile * LANES : (tile + 1) * LANES]
                    )

    def send_blocks(group, lo, hi):
        @pl.loop(0, 16)
        def _(k):
            away = jnp.where(k < 8, PAIRS[group][0], PAIRS[group][1])
            to = ((plane + away) % PLANE) * PLANE + (low + k) % PLANE
            source = send1.at[pl.ds(pl.multiple_of(to * BLOCK + lo * 4, 8), (hi - lo) * 4)]
            target = recv1.at[pl.ds(pl.multiple_of(me * BLOCK + lo * 4, 8), (hi - lo) * 4)]

            @pl.when(to != me)
            def _():
                pltpu.make_async_remote_copy(
                    src_ref=source,
                    dst_ref=target,
                    send_sem=in_send,
                    recv_sem=in_recv,
                    device_id={"comp": to},
                    device_id_type=MESH,
                ).start()

            @pl.when(to == me)
            def _():
                pltpu.make_async_copy(source, target, in_recv).start()

    inner, sides = (0,), (1, 2)
    for step in range(SUBSTEPS - 1):
        for half in range(2):
            finish_rows(step, inner, (half,))
            middle(step, 0, (half,))
            start_rows(step + 1, inner, (half,))
        if step:
            start_dirs(step)
    for half in range(2):
        finish_rows(SUBSTEPS - 1, inner, (half,))
        last(0, (half,))
    send_blocks(0, *INNER)
    for side in range(2):
        for n in range(3):
            dir_copy(side, n).wait()
    mask_first(0, HALO)
    mask_first(HALO + OWN, WIDE)

    @pl.when(south)
    def _():
        for which in range(2):
            diagonal_copy(which, 0).wait_recv()
            diagonal_copy(which, 1).wait_send()

    @pl.when(north)
    def _():
        for which in range(2):
            diagonal_copy(which, 1).wait_recv()
            diagonal_copy(which, 0).wait_send()

    for step in range(SUBSTEPS - 1):
        if step:
            finish_rows(step, sides, (0, 1))
        middle(step, 1)
        middle(step, 2)
        start_rows(step + 1, sides, (0, 1))
        send_blocks(step + 1, *INNER)
    finish_rows(SUBSTEPS - 1, sides)
    last(1)
    last(2)
    for group in range(4):
        send_blocks(group, 0, HALO)
        send_blocks(group, OWN - HALO, OWN)
    wait_bytes(interp, interp_sem)

    @pl.loop(0, COMPS // LANES)
    def _(b):
        span = pl.ds(pl.multiple_of(b * LANES, LANES), LANES)
        store_split(0, span, interp[span, :])
        store_split(1, span, interp[:, span].T)

    wait_bytes(recv1, in_recv)

    @pl.loop(0, COMPS // CHUNK)
    def _(c):
        rows = pl.ds(pl.multiple_of(c * CHUNK, 16), CHUNK)
        for q in range(4):
            value = recv1[pl.ds(c * (CHUNK * 4) + q, CHUNK, stride=4), :]
            at = slice(q * LANES, (q + 1) * LANES)
            high = value.astype(bf16)
            points[rows, at] = value
            points_hi[rows, at] = high
            points_lo[rows, at] = (value - high.astype(f32)).astype(bf16)

    my_group = me // PLANE

    def source_chunk(c, drift):
        group = (plane + plane_offset(c)) % PLANE
        rows = pl.ds(pl.multiple_of(group * CHUNK, 16), CHUNK)
        matrix = jnp.concatenate([split[part, rows, :] for part in range(4)], axis=0)
        both = jnp.dot(matrix, points_hi[...], preferred_element_type=f32)
        more = jnp.dot(matrix[: 2 * CHUNK], points_lo[...], preferred_element_type=f32)
        sums = both[: 2 * CHUNK] + (both[2 * CHUNK :] + more)
        forward, backward = sums[:CHUNK], sums[CHUNK:]
        wave = points[rows, :]
        new = wave + 0.5 * (forward * backward - 0.5 * wave * (forward + backward))
        for q in range(4):
            send2[pl.ds(group * (CHUNK * 4) + q, CHUNK, stride=4), :] = new[:, q * LANES : (q + 1) * LANES]

        @pl.loop(0, PLANE)
        def _(e):
            to = group * PLANE + (low + e) % PLANE

            @pl.when(to != me)
            def _():
                pltpu.make_async_remote_copy(
                    src_ref=block_of(send2, to),
                    dst_ref=block_of(recv2, me),
                    send_sem=out_send,
                    recv_sem=out_recv.at[my_group],
                    device_id={"comp": to},
                    device_id_type=MESH,
                ).start()

            @pl.when(to == me)
            def _():
                pltpu.make_async_copy(
                    block_of(send2, me), block_of(recv2, me), out_recv.at[my_group]
                ).start()

        held = weights[rows, :]
        return tuple(
            drift[a] + jnp.sum((held[:, a : a + 1] * new).reshape(CHUNK // 8, 8, POINTS), axis=0) for a in range(2)
        )

    drift = lax.fori_loop(
        0, PLANE, source_chunk, (jnp.zeros((8, POINTS), f32), jnp.zeros((8, POINTS), f32))
    )
    for a in range(2):
        total = jnp.sum(drift[a], axis=0, keepdims=True)
        for q in range(4):
            drift_block[a * 4 + q : a * 4 + q + 1, :] = total[:, q * LANES : (q + 1) * LANES]

    my_drift = drift_all.at[me]

    @pl.loop(1, TILES)
    def _(t):
        pltpu.make_async_remote_copy(
            src_ref=drift_block,
            dst_ref=my_drift,
            send_sem=drift_send,
            recv_sem=drift_recv,
            device_id={"comp": (me + t) % TILES},
            device_id_type=MESH,
        ).start()

    pltpu.make_async_copy(drift_block, my_drift, drift_recv).start()

    wait_bytes(gathered.at[: TILES - 1], cur_send)
    wait_bytes(recv1.at[: (TILES - 1) * BLOCK], in_send)

    @pl.when(north)
    def _():
        beside_copy(0).wait_send()
        beside_copy(1).wait_recv()

    @pl.when(south)
    def _():
        beside_copy(1).wait_send()
        beside_copy(0).wait_recv()

    @pl.loop(0, PLANE)
    def _(n):
        g = (plane + PLANE - plane_offset(n)) % PLANE
        group_rows = pl.ds(pl.multiple_of(g * PLANE * BLOCK, 8), PLANE * BLOCK)
        wait_bytes(recv2.at[group_rows], out_recv.at[g])

        @pl.loop(0, OWN)
        def _(i):
            for q in range(4):
                cols = pl.ds(pl.multiple_of(g * 4 * LANES + q * LANES, LANES), LANES)
                out[i, :, cols] = recv2[pl.ds(g * PLANE * BLOCK + q + i * 4, ROWS, stride=BLOCK), :]

        cols = pl.ds(pl.multiple_of(g * 4 * LANES, LANES), 4 * LANES)
        pltpu.make_async_copy(out.at[:, :, cols], out_any.at[:, :, cols], store_sem).start()

    wait_bytes(drift_all, drift_recv)
    tile = owner[me]
    row1 = lax.broadcasted_iota(jnp.int32, (ROWS, LANES), 0)

    def twice(value, half):
        other = pltpu.roll(value, 64, 1)
        return jnp.where(half == 0, value, other), jnp.where(half == 0, other, value)

    def mask(which_tile, offset):
        at_left, at_right = twice(masks[offset + 1, which_tile // 2], which_tile % 2)
        return jnp.where(left, at_left, at_right)

    own = mask(tile, 0)
    held = cat[...] * own
    west_tile, east_tile = (tile + TILES - 1) % TILES, (tile + 1) % TILES
    held_w = gathered[inverse[west_tile]] * mask(west_tile, 0)
    held_e = gathered[inverse[east_tile]] * mask(east_tile, 0)
    held_s = jnp.where(south, beside[0] * mask(tile, -1), 0.0)
    held_n = jnp.where(north, beside[1] * mask(tile, 1), 0.0)
    west = jnp.where(lane % 64 == 0, pltpu.roll(held_w, 65, 1), pltpu.roll(held, 1, 1))
    east = jnp.where(lane % 64 == 63, pltpu.roll(held_e, 63, 1), pltpu.roll(held, 127, 1))
    below = jnp.where(row1 == 0, pltpu.roll(held_s, 1, 0), pltpu.roll(held, 1, 0))
    above = jnp.where(row1 == ROWS - 1, pltpu.roll(held_n, 7, 0), pltpu.roll(held, 7, 0))
    lap = west + east + below + above - 4.0 * held
    quarter = (tile % 8) // 2
    sums = [jnp.zeros((ROWS, LANES), f32), jnp.zeros((ROWS, LANES), f32)]
    for r in range(ROWS):
        piece = drift_all[(tile // 8) * ROWS + r]
        for a in range(2):
            chosen = jnp.sum(jnp.where(row1 == quarter + 4 * a, piece, 0.0), axis=0, keepdims=True)
            sums[a] = jnp.where(row1 == r, chosen, sums[a])
    eastward, _ = twice(sums[0], tile % 2)
    _, northward = twice(sums[1], tile % 2)
    stokes = jnp.where(left, eastward, northward)
    turn = jnp.where(left, 1.0, -1.0) * coriolis[rows8, :]
    other = pltpu.roll(held + stokes, 64, 1)
    result = own * (held + 0.5 * (turn * other + 0.2 * lap - 0.1 * held))
    ocean_out[0] = result[:, :64]
    ocean_out[1] = result[:, 64:]

    wait_bytes(drift_all.at[: TILES - 1], drift_send)
    wait_bytes(recv2.at[: (TILES - 1) * BLOCK], out_send)
    wait_bytes(out, store_sem)


def tables():
    angles = np.arange(DIRS, dtype=np.float32) * np.float32(2.0 * math.pi / DIRS)
    cosine, sine = np.cos(angles).astype(np.float32), np.sin(angles).astype(np.float32)
    k = np.arange(COMPS)
    scale = (np.float32(0.2) * (k // DIRS + 1).astype(np.float32) / np.float32(FREQ)).astype(np.float32)
    weights = np.stack([scale * cosine[k % DIRS], scale * sine[k % DIRS]], axis=1)
    latitude = -1.2 + 2.4 * (np.arange(TOTAL_ROWS, dtype=np.float32) + np.float32(0.5)) / TOTAL_ROWS
    coriolis = np.broadcast_to(np.sin(latitude.astype(np.float32))[:, None], (TOTAL_ROWS, LANES))
    return cosine, sine, weights.astype(np.float32), coriolis.astype(np.float32)


def local(spectrum, currents, group_courant, refraction, interp, sea_mask, depth_class, owner_map):
    cosine, sine, weights, coriolis = tables()
    index = jnp.arange(TILES, dtype=jnp.int32)
    inverse = jnp.sum(jnp.where(owner_map[None, :] == index[:, None], index[None, :], 0), axis=1)
    vmem, smem = pl.BlockSpec(memory_space=pltpu.VMEM), pl.BlockSpec(memory_space=pltpu.SMEM)
    anywhere = pl.BlockSpec(memory_space=pl.ANY)
    dma = pltpu.SemaphoreType.DMA
    field = pltpu.VMEM((ROWS, LON), f32)
    blocks = pltpu.VMEM((TILES * BLOCK, LANES), f32)
    edge_rows = pltpu.VMEM((SUBSTEPS, 2, WIDE, 1, LON), f32)
    return pl.pallas_call(
        wave_kernel,
        out_shape=(
            jax.ShapeDtypeStruct((OWN, ROWS, LON), f32),
            jax.ShapeDtypeStruct((2, ROWS, LON // TILES), f32),
        ),
        in_specs=[anywhere, vmem, vmem, vmem, anywhere, vmem, vmem] + [smem] * 6,
        out_specs=(anywhere, vmem),
        scratch_shapes=[
            pltpu.VMEM((SUBSTEPS, WIDE, ROWS, LON), f32),
            edge_rows,
            edge_rows,
            field,
            field,
            field,
            field,
            blocks,
            blocks,
            blocks,
            blocks,
            pltpu.VMEM((OWN, ROWS, LON), f32),
            pltpu.VMEM((COMPS, COMPS), f32),
            pltpu.VMEM((4, COMPS, COMPS), bf16),
            pltpu.VMEM((COMPS, POINTS), f32),
            pltpu.VMEM((COMPS, POINTS), bf16),
            pltpu.VMEM((COMPS, POINTS), bf16),
            pltpu.VMEM((ROWS, LANES), f32),
            pltpu.VMEM((TILES, ROWS, LANES), f32),
            pltpu.VMEM((2, ROWS, LANES), f32),
            pltpu.VMEM((8, LANES), f32),
            pltpu.VMEM((TILES, 8, LANES), f32),
            pltpu.VMEM((3, LON // LANES, ROWS, LANES), f32),
            dma,
            dma,
            dma,
            dma,
            dma((2,)),
            dma((2,)),
            dma((SUBSTEPS, 3, 2, 2)),
            dma((SUBSTEPS, 3, 2, 2)),
            dma((2, 3)),
            dma((2, 3)),
            dma,
            dma,
            dma,
            dma((PLANE,)),
            dma,
            dma,
            dma,
        ],
        compiler_params=pltpu.CompilerParams(
            collective_id=0, has_side_effects=True, vmem_limit_bytes=62 * 2**20
        ),
        name="waves",
    )(
        spectrum, currents, sea_mask, depth_class, interp, jnp.asarray(weights), jnp.asarray(coriolis), group_courant,
        refraction, owner_map, inverse, jnp.asarray(cosine), jnp.asarray(sine),
    )


def solution(mesh):
    in_specs = (P("comp", "band", None), P(None, "band", "comp"), P(), P(), P(), P(), P(), P())
    out_specs = (P("comp", "band", None), P(None, "band", "comp"))
    return jax.shard_map(local, mesh=mesh, in_specs=in_specs, out_specs=out_specs, check_vma=False)
```

```python
import math

import jax
import jax.numpy as jnp
import numpy as np
from jax import lax
from jax.experimental import pallas as pl
from jax.experimental.pallas import tpu as pltpu
from jax.sharding import PartitionSpec as P

DIRS = 36
FREQ = 32
CLASSES = 8
SUBSTEPS = 4
COMPS = 1152
OWN = 18
ROWS = 8
TOTAL_ROWS = 32
LON = 4096
TILES = 64
PLANE = 8
LANES = 128
BLOCK = OWN * 4
CHUNK = 144
POINTS = 512
PIECE = 1024
HALF = 1024
HALO = 4
WIDE = OWN + 2 * HALO
PAIRS = ((4, 0), (3, 7), (5, 1), (2, 6))
INNER = (4, 14)
MESH = pl.DeviceIdType.MESH
f32 = jnp.float32
bf16 = jnp.bfloat16


def plane_offset(step):
    return 3 * (step + 1) % PLANE


def block_of(ref, which):
    return ref.at[pl.ds(pl.multiple_of(which * BLOCK, 8), BLOCK)]


def wait_bytes(ref, sem):
    pltpu.make_async_copy(ref, ref, sem).wait()


def wave_kernel(
    spectrum_any, currents, sea, classes, interp_any, weights, coriolis, courant, refraction, owner, inverse, cosine, sine,
    out_any, ocean_out,
    state, rows_out, rows_in, base_u, base_v, turning, ocean, send1, recv1, send2, recv2, out, interp, split,
    points, points_hi, points_lo, cat, gathered, beside, drift_block, drift_all, masks,
    interp_sem, spec_sem, cur_send, cur_recv, beside_send, beside_recv, row_send, row_recv, dir_send, dir_recv,
    in_send, in_recv, out_send, out_recv, drift_send, drift_recv, store_sem,
):
    me = lax.axis_index("comp")
    band = lax.axis_index("band")
    plane = me // PLANE
    low = me % PLANE
    partner = me + 1 - 2 * (me % 2)
    freq = me // 2
    first_dir = (me % 2) * OWN
    south = band > 0
    north = band < 3

    for n in range(0, OWN, 3):
        pltpu.make_async_copy(spectrum_any.at[n : n + 3], state.at[0, HALO + n : HALO + n + 3], spec_sem).start()

    barrier = pltpu.get_barrier_semaphore()

    @pl.loop(1, TILES)
    def _(t):
        pl.semaphore_signal(barrier, inc=1, device_id={"comp": (me + t) % TILES}, device_id_type=MESH)

    @pl.when(south)
    def _():
        pl.semaphore_signal(barrier, inc=1, device_id={"band": band - 1}, device_id_type=MESH)
        pl.semaphore_signal(barrier, inc=1, device_id={"comp": partner, "band": band - 1}, device_id_type=MESH)

    @pl.when(north)
    def _():
        pl.semaphore_signal(barrier, inc=1, device_id={"band": band + 1}, device_id_type=MESH)
        pl.semaphore_signal(barrier, inc=1, device_id={"comp": partner, "band": band + 1}, device_id_type=MESH)

    rows8 = pl.ds(pl.multiple_of(band * ROWS, ROWS), ROWS)

    ocean[...] = sea[rows8, :].astype(f32)
    cat[:, :64] = currents[0]
    cat[:, 64:] = currents[1]

    def span(step, part):
        return ((5 + step, 21 - step), (1 + step, 5 + step), (21 - step, 25 - step))[part]

    def row_copy(step, part, half, side):
        lo, hi = span(step, part) if step else (HALO, HALO + OWN)
        cols = slice(half * HALF, (half + 1) * HALF)
        return pltpu.make_async_remote_copy(
            src_ref=rows_out.at[step, side, lo:hi, :, cols],
            dst_ref=rows_in.at[step, side, lo:hi, :, cols],
            send_sem=row_send.at[step, part, half, side],
            recv_sem=row_recv.at[step, part, half, side],
            device_id={"band": band + 1 - 2 * side},
            device_id_type=MESH,
        )

    def start_rows(step, parts, halves=(0, 1, 2, 3)):
        @pl.when(north)
        def _():
            for part in parts:
                for half in halves:
                    row_copy(step, part, half, 0).start()

        @pl.when(south)
        def _():
            for part in parts:
                for half in halves:
                    row_copy(step, part, half, 1).start()

    def finish_rows(step, parts, halves=(0, 1, 2, 3)):
        @pl.when(south)
        def _():
            for part in parts:
                for half in halves:
                    row_copy(step, part, half, 0).wait_recv()
                    row_copy(step, part, half, 1).wait_send()

        @pl.when(north)
        def _():
            for part in parts:
                for half in halves:
                    row_copy(step, part, half, 1).wait_recv()
                    row_copy(step, part, half, 0).wait_send()

    def diagonal_copy(which, side):
        lo, to = ((19, 1), (4, 22))[which]
        return pltpu.make_async_remote_copy(
            src_ref=rows_out.at[0, side, lo : lo + 3],
            dst_ref=rows_in.at[0, side, to : to + 3],
            send_sem=row_send.at[0, 1 + which, 0, side],
            recv_sem=row_recv.at[0, 1 + which, 0, side],
            device_id={"comp": partner, "band": band + 1 - 2 * side},
            device_id_type=MESH,
        )

    pieces = ((0, 2), (2, 3), (3, 4))

    def dir_copy(side, n):
        lo, hi = pieces[n]
        source = (OWN - HALO if side == 0 else 0) + lo
        to = (0 if side == 0 else HALO + OWN) + lo
        return pltpu.make_async_remote_copy(
            src_ref=spectrum_any.at[source : source + hi - lo],
            dst_ref=state.at[0, to : to + hi - lo],
            send_sem=dir_send.at[side, n],
            recv_sem=dir_recv.at[side, n],
            device_id={"comp": partner},
            device_id_type=MESH,
        )

    def start_dirs(n):
        dir_copy(0, n).start()
        dir_copy(1, n).start()

    def mask_first(lo, hi):
        @pl.loop(lo, hi)
        def _(e):
            masked = state[0, e] * ocean[...]
            state[0, e] = masked
            if lo == HALO:
                rows_out[0, 0, e] = masked[ROWS - 1 :, :]
                rows_out[0, 1, e] = masked[:1, :]

    wait_bytes(state.at[0, HALO : HALO + OWN], spec_sem)
    mask_first(HALO, HALO + OWN)
    pl.semaphore_wait(barrier, TILES - 1 + jnp.where(south, 2, 0) + jnp.where(north, 2, 0))

    def cur_copy(t):
        return pltpu.make_async_remote_copy(
            src_ref=cat,
            dst_ref=gathered.at[me],
            send_sem=cur_send,
            recv_sem=cur_recv,
            device_id={"comp": (me + t) % TILES},
            device_id_type=MESH,
        )

    def beside_copy(side):
        return pltpu.make_async_remote_copy(
            src_ref=cat,
            dst_ref=beside.at[side],
            send_sem=beside_send.at[side],
            recv_sem=beside_recv.at[side],
            device_id={"band": band + 1 - 2 * side},
            device_id_type=MESH,
        )

    start_rows(0, (0,))

    @pl.loop(1, TILES)
    def _(t):
        cur_copy(t).start()

    pltpu.make_async_copy(cat, gathered.at[me], cur_recv).start()

    start_dirs(0)
    for n in range(0, COMPS, LANES):
        pltpu.make_async_copy(interp_any.at[n : n + LANES], interp.at[n : n + LANES], interp_sem).start()

    @pl.when(north)
    def _():
        beside_copy(0).start()
        diagonal_copy(0, 0).start()
        diagonal_copy(1, 0).start()

    @pl.when(south)
    def _():
        beside_copy(1).start()
        diagonal_copy(0, 1).start()
        diagonal_copy(1, 1).start()

    @pl.when(band == 0)
    def _():
        rows_in[:, 0] = jnp.zeros((SUBSTEPS, WIDE, 1, LON), f32)

    @pl.when(band == 3)
    def _():
        rows_in[:, 1] = jnp.zeros((SUBSTEPS, WIDE, 1, LON), f32)

    own_class = classes[rows8, :]
    turned = jnp.zeros((ROWS, LON), f32)
    for level in range(CLASSES):
        turned = jnp.where(own_class == level, refraction[level, freq], turned)
    turning[...] = turned

    for offset in range(3):
        there = jnp.minimum(jnp.maximum(band + offset - 1, 0), 3)
        for col in range(LON // LANES):
            masks[offset, col] = sea[
                pl.ds(pl.multiple_of(there * ROWS, ROWS), ROWS), col * LANES : (col + 1) * LANES
            ].astype(f32)

    def store_split(part, rows, value):
        high = value.astype(bf16)
        split[part, rows, :] = high
        split[2 + part, rows, :] = (value - high.astype(f32)).astype(bf16)

    wait_bytes(gathered, cur_recv)

    lane = lax.broadcasted_iota(jnp.int32, (ROWS, LANES), 1)
    left = lane < 64
    for u in range(TILES // 2):
        one = gathered[inverse[2 * u]]
        two = gathered[inverse[2 * u + 1]]
        east_part = 0.025 * jnp.where(left, one, pltpu.roll(two, 64, 1))
        north_part = 0.025 * jnp.where(left, pltpu.roll(one, 64, 1), two)
        at = slice(u * LANES, (u + 1) * LANES)
        base_u[:, at] = east_part
        base_v[:, at] = north_part

    row = lax.broadcasted_iota(jnp.int32, (ROWS, PIECE), 0)
    speed = courant[freq]

    def advanced(step, e, piece):
        lo = piece * PIECE
        at = slice(lo, lo + PIECE)
        centre = state[step, e, :, at]
        west_lo, east_lo = (lo - LANES) % LON, (lo + PIECE) % LON
        west_piece = state[step, e, :, west_lo : west_lo + LANES]
        east_piece = state[step, e, :, east_lo : east_lo + LANES]
        wide = jnp.concatenate([west_piece, centre, east_piece], axis=1)
        west = pltpu.roll(wide, 1, 1)[:, LANES:-LANES]
        east = pltpu.roll(wide, PIECE + 2 * LANES - 1, 1)[:, LANES:-LANES]
        below = jnp.where(row == 0, rows_in[step, 0, e, :, at], pltpu.roll(centre, 1, 0))
        above = jnp.where(row == ROWS - 1, rows_in[step, 1, e, :, at], pltpu.roll(centre, ROWS - 1, 0))
        before = state[step, e - 1, :, at]
        after = state[step, e + 1, :, at]
        direction = (first_dir + e + DIRS - HALO) % DIRS
        cos_d = cosine[direction]
        ax = base_u[:, at] + speed * cos_d
        ay = base_v[:, at] + speed * sine[direction]
        turn = turning[:, at] * cos_d
        change = (
            ax * jnp.where(ax > 0.0, centre - west, east - centre)
            + ay * jnp.where(ay > 0.0, centre - below, above - centre)
            + turn * jnp.where(turn > 0.0, centre - before, after - centre)
        )
        return ocean[:, at] * (centre - change)

    def middle(step, part, halves=(0, 1, 2, 3)):
        lo, hi = span(step, part)

        @pl.loop(lo, hi)
        def _(e):
            for piece in range(halves[0], halves[-1] + 1):
                at = slice(piece * PIECE, (piece + 1) * PIECE)
                new = advanced(step, e, piece)
                state[step + 1, e, :, at] = new
                rows_out[step + 1, 0, e, :, at] = new[ROWS - 1 :, :]
                rows_out[step + 1, 1, e, :, at] = new[:1, :]

    def last(part, halves=(0, 1, 2, 3)):
        lo, hi = span(SUBSTEPS - 1, part)

        @pl.loop(lo, hi)
        def _(e):
            for piece in range(halves[0], halves[-1] + 1):
                new = advanced(SUBSTEPS - 1, e, piece)
                for tile in range(PIECE // LANES):
                    col = piece * (PIECE // LANES) + tile
                    first = (col // 4) * ROWS * BLOCK + col % 4
                    send1[pl.ds(first + (e - HALO) * 4, ROWS, stride=BLOCK), :] = (
                        new[:, tile * LANES : (tile + 1) * LANES]
                    )

    def send_blocks(group, lo, hi):
        @pl.loop(0, 16)
        def _(k):
            away = jnp.where(k < 8, PAIRS[group][0], PAIRS[group][1])
            to = ((plane + away) % PLANE) * PLANE + (low + k) % PLANE
            source = send1.at[pl.ds(pl.multiple_of(to * BLOCK + lo * 4, 8), (hi - lo) * 4)]
            target = recv1.at[pl.ds(pl.multiple_of(me * BLOCK + lo * 4, 8), (hi - lo) * 4)]

            @pl.when(to != me)
            def _():
                pltpu.make_async_remote_copy(
                    src_ref=source,
                    dst_ref=target,
                    send_sem=in_send,
                    recv_sem=in_recv,
                    device_id={"comp": to},
                    device_id_type=MESH,
                ).start()

            @pl.when(to == me)
            def _():
                pltpu.make_async_copy(source, target, in_recv).start()

    inner, sides = (0,), (1, 2)
    for step in range(SUBSTEPS - 1):
        for half in range(4):
            finish_rows(step, inner, (half,))
            middle(step, 0, (half,))
            start_rows(step + 1, inner, (half,))
        if step:
            start_dirs(step)
    for half in range(4):
        finish_rows(SUBSTEPS - 1, inner, (half,))
        last(0, (half,))
    send_blocks(0, *INNER)
    for side in range(2):
        for n in range(3):
            dir_copy(side, n).wait()
    mask_first(0, HALO)
    mask_first(HALO + OWN, WIDE)

    @pl.when(south)
    def _():
        for which in range(2):
            diagonal_copy(which, 0).wait_recv()
            diagonal_copy(which, 1).wait_send()

    @pl.when(north)
    def _():
        for which in range(2):
            diagonal_copy(which, 1).wait_recv()
            diagonal_copy(which, 0).wait_send()

    for step in range(SUBSTEPS - 1):
        if step:
            finish_rows(step, sides, (0, 1, 2, 3))
        middle(step, 1)
        middle(step, 2)
        start_rows(step + 1, sides, (0, 1, 2, 3))
        send_blocks(step + 1, *INNER)
    finish_rows(SUBSTEPS - 1, sides)
    last(1)
    last(2)
    for group in range(4):
        send_blocks(group, 0, HALO)
        send_blocks(group, OWN - HALO, OWN)
    wait_bytes(interp, interp_sem)

    @pl.loop(0, COMPS // LANES)
    def _(b):
        span = pl.ds(pl.multiple_of(b * LANES, LANES), LANES)
        store_split(0, span, interp[span, :])
        store_split(1, span, interp[:, span].T)

    wait_bytes(recv1, in_recv)

    @pl.loop(0, COMPS // CHUNK)
    def _(c):
        rows = pl.ds(pl.multiple_of(c * CHUNK, 16), CHUNK)
        for q in range(4):
            value = recv1[pl.ds(c * (CHUNK * 4) + q, CHUNK, stride=4), :]
            at = slice(q * LANES, (q + 1) * LANES)
            high = value.astype(bf16)
            points[rows, at] = value
            points_hi[rows, at] = high
            points_lo[rows, at] = (value - high.astype(f32)).astype(bf16)

    my_group = me // PLANE

    def source_chunk(c, drift):
        group = (plane + plane_offset(c)) % PLANE
        rows = pl.ds(pl.multiple_of(group * CHUNK, 16), CHUNK)
        matrix = jnp.concatenate([split[part, rows, :] for part in range(4)], axis=0)
        both = jnp.dot(matrix, points_hi[...], preferred_element_type=f32)
        more = jnp.dot(matrix[: 2 * CHUNK], points_lo[...], preferred_element_type=f32)
        sums = both[: 2 * CHUNK] + (both[2 * CHUNK :] + more)
        forward, backward = sums[:CHUNK], sums[CHUNK:]
        wave = points[rows, :]
        new = wave + 0.5 * (forward * backward - 0.5 * wave * (forward + backward))
        for q in range(4):
            send2[pl.ds(group * (CHUNK * 4) + q, CHUNK, stride=4), :] = new[:, q * LANES : (q + 1) * LANES]

        @pl.loop(0, PLANE)
        def _(e):
            to = group * PLANE + (low + e) % PLANE

            @pl.when(to != me)
            def _():
                pltpu.make_async_remote_copy(
                    src_ref=block_of(send2, to),
                    dst_ref=block_of(recv2, me),
                    send_sem=out_send,
                    recv_sem=out_recv.at[my_group],
                    device_id={"comp": to},
                    device_id_type=MESH,
                ).start()

            @pl.when(to == me)
            def _():
                pltpu.make_async_copy(
                    block_of(send2, me), block_of(recv2, me), out_recv.at[my_group]
                ).start()

        held = weights[rows, :]
        return tuple(
            drift[a] + jnp.sum((held[:, a : a + 1] * new).reshape(CHUNK // 8, 8, POINTS), axis=0) for a in range(2)
        )

    drift = lax.fori_loop(
        0, PLANE, source_chunk, (jnp.zeros((8, POINTS), f32), jnp.zeros((8, POINTS), f32))
    )
    for a in range(2):
        total = jnp.sum(drift[a], axis=0, keepdims=True)
        for q in range(4):
            drift_block[a * 4 + q : a * 4 + q + 1, :] = total[:, q * LANES : (q + 1) * LANES]

    my_drift = drift_all.at[me]

    @pl.loop(1, TILES)
    def _(t):
        pltpu.make_async_remote_copy(
            src_ref=drift_block,
            dst_ref=my_drift,
            send_sem=drift_send,
            recv_sem=drift_recv,
            device_id={"comp": (me + t) % TILES},
            device_id_type=MESH,
        ).start()

    pltpu.make_async_copy(drift_block, my_drift, drift_recv).start()

    wait_bytes(gathered.at[: TILES - 1], cur_send)
    wait_bytes(recv1.at[: (TILES - 1) * BLOCK], in_send)

    @pl.when(north)
    def _():
        beside_copy(0).wait_send()
        beside_copy(1).wait_recv()

    @pl.when(south)
    def _():
        beside_copy(1).wait_send()
        beside_copy(0).wait_recv()

    @pl.loop(0, PLANE)
    def _(n):
        g = (plane + PLANE - plane_offset(n)) % PLANE
        group_rows = pl.ds(pl.multiple_of(g * PLANE * BLOCK, 8), PLANE * BLOCK)
        wait_bytes(recv2.at[group_rows], out_recv.at[g])

        @pl.loop(0, OWN)
        def _(i):
            for q in range(4):
                cols = pl.ds(pl.multiple_of(g * 4 * LANES + q * LANES, LANES), LANES)
                out[i, :, cols] = recv2[pl.ds(g * PLANE * BLOCK + q + i * 4, ROWS, stride=BLOCK), :]

        cols = pl.ds(pl.multiple_of(g * 4 * LANES, LANES), 4 * LANES)
        pltpu.make_async_copy(out.at[:, :, cols], out_any.at[:, :, cols], store_sem).start()

    wait_bytes(drift_all, drift_recv)
    tile = owner[me]
    row1 = lax.broadcasted_iota(jnp.int32, (ROWS, LANES), 0)

    def twice(value, half):
        other = pltpu.roll(value, 64, 1)
        return jnp.where(half == 0, value, other), jnp.where(half == 0, other, value)

    def mask(which_tile, offset):
        at_left, at_right = twice(masks[offset + 1, which_tile // 2], which_tile % 2)
        return jnp.where(left, at_left, at_right)

    own = mask(tile, 0)
    held = cat[...] * own
    west_tile, east_tile = (tile + TILES - 1) % TILES, (tile + 1) % TILES
    held_w = gathered[inverse[west_tile]] * mask(west_tile, 0)
    held_e = gathered[inverse[east_tile]] * mask(east_tile, 0)
    held_s = jnp.where(south, beside[0] * mask(tile, -1), 0.0)
    held_n = jnp.where(north, beside[1] * mask(tile, 1), 0.0)
    west = jnp.where(lane % 64 == 0, pltpu.roll(held_w, 65, 1), pltpu.roll(held, 1, 1))
    east = jnp.where(lane % 64 == 63, pltpu.roll(held_e, 63, 1), pltpu.roll(held, 127, 1))
    below = jnp.where(row1 == 0, pltpu.roll(held_s, 1, 0), pltpu.roll(held, 1, 0))
    above = jnp.where(row1 == ROWS - 1, pltpu.roll(held_n, 7, 0), pltpu.roll(held, 7, 0))
    lap = west + east + below + above - 4.0 * held
    quarter = (tile % 8) // 2
    sums = [jnp.zeros((ROWS, LANES), f32), jnp.zeros((ROWS, LANES), f32)]
    for r in range(ROWS):
        piece = drift_all[(tile // 8) * ROWS + r]
        for a in range(2):
            chosen = jnp.sum(jnp.where(row1 == quarter + 4 * a, piece, 0.0), axis=0, keepdims=True)
            sums[a] = jnp.where(row1 == r, chosen, sums[a])
    eastward, _ = twice(sums[0], tile % 2)
    _, northward = twice(sums[1], tile % 2)
    stokes = jnp.where(left, eastward, northward)
    turn = jnp.where(left, 1.0, -1.0) * coriolis[rows8, :]
    other = pltpu.roll(held + stokes, 64, 1)
    result = own * (held + 0.5 * (turn * other + 0.2 * lap - 0.1 * held))
    ocean_out[0] = result[:, :64]
    ocean_out[1] = result[:, 64:]

    wait_bytes(drift_all.at[: TILES - 1], drift_send)
    wait_bytes(recv2.at[: (TILES - 1) * BLOCK], out_send)
    wait_bytes(out, store_sem)


def tables():
    angles = np.arange(DIRS, dtype=np.float32) * np.float32(2.0 * math.pi / DIRS)
    cosine, sine = np.cos(angles).astype(np.float32), np.sin(angles).astype(np.float32)
    k = np.arange(COMPS)
    scale = (np.float32(0.2) * (k // DIRS + 1).astype(np.float32) / np.float32(FREQ)).astype(np.float32)
    weights = np.stack([scale * cosine[k % DIRS], scale * sine[k % DIRS]], axis=1)
    latitude = -1.2 + 2.4 * (np.arange(TOTAL_ROWS, dtype=np.float32) + np.float32(0.5)) / TOTAL_ROWS
    coriolis = np.broadcast_to(np.sin(latitude.astype(np.float32))[:, None], (TOTAL_ROWS, LANES))
    return cosine, sine, weights.astype(np.float32), coriolis.astype(np.float32)


def local(spectrum, currents, group_courant, refraction, interp, sea_mask, depth_class, owner_map):
    cosine, sine, weights, coriolis = tables()
    index = jnp.arange(TILES, dtype=jnp.int32)
    inverse = jnp.sum(jnp.where(owner_map[None, :] == index[:, None], index[None, :], 0), axis=1)
    vmem, smem = pl.BlockSpec(memory_space=pltpu.VMEM), pl.BlockSpec(memory_space=pltpu.SMEM)
    anywhere = pl.BlockSpec(memory_space=pl.ANY)
    dma = pltpu.SemaphoreType.DMA
    field = pltpu.VMEM((ROWS, LON), f32)
    blocks = pltpu.VMEM((TILES * BLOCK, LANES), f32)
    edge_rows = pltpu.VMEM((SUBSTEPS, 2, WIDE, 1, LON), f32)
    return pl.pallas_call(
        wave_kernel,
        out_shape=(
            jax.ShapeDtypeStruct((OWN, ROWS, LON), f32),
            jax.ShapeDtypeStruct((2, ROWS, LON // TILES), f32),
        ),
        in_specs=[anywhere, vmem, vmem, vmem, anywhere, vmem, vmem] + [smem] * 6,
        out_specs=(anywhere, vmem),
        scratch_shapes=[
            pltpu.VMEM((SUBSTEPS, WIDE, ROWS, LON), f32),
            edge_rows,
            edge_rows,
            field,
            field,
            field,
            field,
            blocks,
            blocks,
            blocks,
            blocks,
            pltpu.VMEM((OWN, ROWS, LON), f32),
            pltpu.VMEM((COMPS, COMPS), f32),
            pltpu.VMEM((4, COMPS, COMPS), bf16),
            pltpu.VMEM((COMPS, POINTS), f32),
            pltpu.VMEM((COMPS, POINTS), bf16),
            pltpu.VMEM((COMPS, POINTS), bf16),
            pltpu.VMEM((ROWS, LANES), f32),
            pltpu.VMEM((TILES, ROWS, LANES), f32),
            pltpu.VMEM((2, ROWS, LANES), f32),
            pltpu.VMEM((8, LANES), f32),
            pltpu.VMEM((TILES, 8, LANES), f32),
            pltpu.VMEM((3, LON // LANES, ROWS, LANES), f32),
            dma,
            dma,
            dma,
            dma,
            dma((2,)),
            dma((2,)),
            dma((SUBSTEPS, 3, 4, 2)),
            dma((SUBSTEPS, 3, 4, 2)),
            dma((2, 3)),
            dma((2, 3)),
            dma,
            dma,
            dma,
            dma((PLANE,)),
            dma,
            dma,
            dma,
        ],
        compiler_params=pltpu.CompilerParams(
            collective_id=0, has_side_effects=True, vmem_limit_bytes=62 * 2**20
        ),
        name="waves",
    )(
        spectrum, currents, sea_mask, depth_class, interp, jnp.asarray(weights), jnp.asarray(coriolis), group_courant,
        refraction, owner_map, inverse, jnp.asarray(cosine), jnp.asarray(sine),
    )


def solution(mesh):
    in_specs = (P("comp", "band", None), P(None, "band", "comp"), P(), P(), P(), P(), P(), P())
    out_specs = (P("comp", "band", None), P(None, "band", "comp"))
    return jax.shard_map(local, mesh=mesh, in_specs=in_specs, out_specs=out_specs, check_vma=False)
```

```python
import math

import jax
import jax.numpy as jnp
import numpy as np
from jax import lax
from jax.experimental import pallas as pl
from jax.experimental.pallas import tpu as pltpu
from jax.sharding import PartitionSpec as P

DIRS = 36
FREQ = 32
CLASSES = 8
SUBSTEPS = 4
COMPS = 1152
OWN = 18
ROWS = 8
TOTAL_ROWS = 32
LON = 4096
TILES = 64
PLANE = 8
LANES = 128
BLOCK = OWN * 4
CHUNK = 144
POINTS = 512
PIECE = 1024
HALF = 1024
HALO = 4
WIDE = OWN + 2 * HALO
PAIRS = ((4, 0), (3, 7), (5, 1), (2, 6))
INNER = (4, 14)
MESH = pl.DeviceIdType.MESH
f32 = jnp.float32
bf16 = jnp.bfloat16


def plane_offset(step):
    return 3 * (step + 1) % PLANE


def block_of(ref, which):
    return ref.at[pl.ds(pl.multiple_of(which * BLOCK, 8), BLOCK)]


def wait_bytes(ref, sem):
    pltpu.make_async_copy(ref, ref, sem).wait()


def wave_kernel(
    spectrum_any, currents, sea, classes, interp_any, weights, coriolis, courant, refraction, owner, inverse, cosine, sine,
    out_any, ocean_out,
    state, rows_out, rows_in, base_u, base_v, turning, ocean, send1, recv1, send2, recv2, out, interp, split,
    points, points_hi, points_lo, cat, gathered, beside, drift_block, drift_all, masks,
    interp_sem, spec_sem, cur_send, cur_recv, beside_send, beside_recv, row_send, row_recv, dir_send, dir_recv,
    in_send, in_recv, out_send, out_recv, drift_send, drift_recv, store_sem,
):
    me = lax.axis_index("comp")
    band = lax.axis_index("band")
    plane = me // PLANE
    low = me % PLANE
    partner = me + 1 - 2 * (me % 2)
    freq = me // 2
    first_dir = (me % 2) * OWN
    south = band > 0
    north = band < 3

    for n in range(0, OWN, 3):
        pltpu.make_async_copy(spectrum_any.at[n : n + 3], state.at[0, HALO + n : HALO + n + 3], spec_sem).start()

    barrier = pltpu.get_barrier_semaphore()

    @pl.loop(1, TILES)
    def _(t):
        pl.semaphore_signal(barrier, inc=1, device_id={"comp": (me + t) % TILES}, device_id_type=MESH)

    @pl.when(south)
    def _():
        pl.semaphore_signal(barrier, inc=1, device_id={"band": band - 1}, device_id_type=MESH)
        pl.semaphore_signal(barrier, inc=1, device_id={"comp": partner, "band": band - 1}, device_id_type=MESH)

    @pl.when(north)
    def _():
        pl.semaphore_signal(barrier, inc=1, device_id={"band": band + 1}, device_id_type=MESH)
        pl.semaphore_signal(barrier, inc=1, device_id={"comp": partner, "band": band + 1}, device_id_type=MESH)

    rows8 = pl.ds(pl.multiple_of(band * ROWS, ROWS), ROWS)

    ocean[...] = sea[rows8, :].astype(f32)
    cat[:, :64] = currents[0]
    cat[:, 64:] = currents[1]

    def span(step, part):
        return ((5 + step, 21 - step), (1 + step, 5 + step), (21 - step, 25 - step))[part]

    def row_copy(step, part, half, side):
        lo, hi = span(step, part) if step else (HALO, HALO + OWN)
        cols = slice(half * HALF, (half + 1) * HALF)
        return pltpu.make_async_remote_copy(
            src_ref=rows_out.at[step, side, lo:hi, :, cols],
            dst_ref=rows_in.at[step, side, lo:hi, :, cols],
            send_sem=row_send.at[step, part, half, side],
            recv_sem=row_recv.at[step, part, half, side],
            device_id={"band": band + 1 - 2 * side},
            device_id_type=MESH,
        )

    def start_rows(step, parts, halves=(0, 1, 2, 3)):
        @pl.when(north)
        def _():
            for part in parts:
                for half in halves:
                    row_copy(step, part, half, 0).start()

        @pl.when(south)
        def _():
            for part in parts:
                for half in halves:
                    row_copy(step, part, half, 1).start()

    def finish_rows(step, parts, halves=(0, 1, 2, 3)):
        @pl.when(south)
        def _():
            for part in parts:
                for half in halves:
                    row_copy(step, part, half, 0).wait_recv()
                    row_copy(step, part, half, 1).wait_send()

        @pl.when(north)
        def _():
            for part in parts:
                for half in halves:
                    row_copy(step, part, half, 1).wait_recv()
                    row_copy(step, part, half, 0).wait_send()

    def diagonal_copy(which, side):
        lo, to = ((19, 1), (4, 22))[which]
        return pltpu.make_async_remote_copy(
            src_ref=rows_out.at[0, side, lo : lo + 3],
            dst_ref=rows_in.at[0, side, to : to + 3],
            send_sem=row_send.at[0, 1 + which, 0, side],
            recv_sem=row_recv.at[0, 1 + which, 0, side],
            device_id={"comp": partner, "band": band + 1 - 2 * side},
            device_id_type=MESH,
        )

    pieces = ((0, 2), (2, 3), (3, 4))

    def dir_copy(side, n):
        lo, hi = pieces[n]
        source = (OWN - HALO if side == 0 else 0) + lo
        to = (0 if side == 0 else HALO + OWN) + lo
        return pltpu.make_async_remote_copy(
            src_ref=spectrum_any.at[source : source + hi - lo],
            dst_ref=state.at[0, to : to + hi - lo],
            send_sem=dir_send.at[side, n],
            recv_sem=dir_recv.at[side, n],
            device_id={"comp": partner},
            device_id_type=MESH,
        )

    def start_dirs(n):
        dir_copy(0, n).start()
        dir_copy(1, n).start()

    def mask_first(lo, hi):
        @pl.loop(lo, hi)
        def _(e):
            masked = state[0, e] * ocean[...]
            state[0, e] = masked
            if lo == HALO:
                rows_out[0, 0, e] = masked[ROWS - 1 :, :]
                rows_out[0, 1, e] = masked[:1, :]

    wait_bytes(state.at[0, HALO : HALO + OWN], spec_sem)
    mask_first(HALO, HALO + OWN)
    pl.semaphore_wait(barrier, TILES - 1 + jnp.where(south, 2, 0) + jnp.where(north, 2, 0))

    def cur_copy(t):
        return pltpu.make_async_remote_copy(
            src_ref=cat,
            dst_ref=gathered.at[me],
            send_sem=cur_send,
            recv_sem=cur_recv,
            device_id={"comp": (me + t) % TILES},
            device_id_type=MESH,
        )

    def beside_copy(side):
        return pltpu.make_async_remote_copy(
            src_ref=cat,
            dst_ref=beside.at[side],
            send_sem=beside_send.at[side],
            recv_sem=beside_recv.at[side],
            device_id={"band": band + 1 - 2 * side},
            device_id_type=MESH,
        )


    @pl.loop(1, TILES)
    def _(t):
        cur_copy(t).start()

    pltpu.make_async_copy(cat, gathered.at[me], cur_recv).start()
    start_rows(0, (0,))

    start_dirs(0)

    @pl.when(north)
    def _():
        beside_copy(0).start()
        diagonal_copy(0, 0).start()
        diagonal_copy(1, 0).start()

    @pl.when(south)
    def _():
        beside_copy(1).start()
        diagonal_copy(0, 1).start()
        diagonal_copy(1, 1).start()

    @pl.when(band == 0)
    def _():
        rows_in[:, 0] = jnp.zeros((SUBSTEPS, WIDE, 1, LON), f32)

    @pl.when(band == 3)
    def _():
        rows_in[:, 1] = jnp.zeros((SUBSTEPS, WIDE, 1, LON), f32)

    own_class = classes[rows8, :]
    turned = jnp.zeros((ROWS, LON), f32)
    for level in range(CLASSES):
        turned = jnp.where(own_class == level, refraction[level, freq], turned)
    turning[...] = turned

    for offset in range(3):
        there = jnp.minimum(jnp.maximum(band + offset - 1, 0), 3)
        for col in range(LON // LANES):
            masks[offset, col] = sea[
                pl.ds(pl.multiple_of(there * ROWS, ROWS), ROWS), col * LANES : (col + 1) * LANES
            ].astype(f32)

    def store_split(part, rows, value):
        high = value.astype(bf16)
        split[part, rows, :] = high
        split[2 + part, rows, :] = (value - high.astype(f32)).astype(bf16)

    wait_bytes(gathered, cur_recv)

    lane = lax.broadcasted_iota(jnp.int32, (ROWS, LANES), 1)
    left = lane < 64
    for u in range(TILES // 2):
        one = gathered[inverse[2 * u]]
        two = gathered[inverse[2 * u + 1]]
        east_part = 0.025 * jnp.where(left, one, pltpu.roll(two, 64, 1))
        north_part = 0.025 * jnp.where(left, pltpu.roll(one, 64, 1), two)
        at = slice(u * LANES, (u + 1) * LANES)
        base_u[:, at] = east_part
        base_v[:, at] = north_part

    row = lax.broadcasted_iota(jnp.int32, (ROWS, PIECE), 0)
    speed = courant[freq]

    def advanced(step, e, piece):
        lo = piece * PIECE
        at = slice(lo, lo + PIECE)
        centre = state[step, e, :, at]
        west_lo, east_lo = (lo - LANES) % LON, (lo + PIECE) % LON
        west_piece = state[step, e, :, west_lo : west_lo + LANES]
        east_piece = state[step, e, :, east_lo : east_lo + LANES]
        wide = jnp.concatenate([west_piece, centre, east_piece], axis=1)
        west = pltpu.roll(wide, 1, 1)[:, LANES:-LANES]
        east = pltpu.roll(wide, PIECE + 2 * LANES - 1, 1)[:, LANES:-LANES]
        below = jnp.where(row == 0, rows_in[step, 0, e, :, at], pltpu.roll(centre, 1, 0))
        above = jnp.where(row == ROWS - 1, rows_in[step, 1, e, :, at], pltpu.roll(centre, ROWS - 1, 0))
        before = state[step, e - 1, :, at]
        after = state[step, e + 1, :, at]
        direction = (first_dir + e + DIRS - HALO) % DIRS
        cos_d = cosine[direction]
        ax = base_u[:, at] + speed * cos_d
        ay = base_v[:, at] + speed * sine[direction]
        turn = turning[:, at] * cos_d
        change = (
            ax * jnp.where(ax > 0.0, centre - west, east - centre)
            + ay * jnp.where(ay > 0.0, centre - below, above - centre)
            + turn * jnp.where(turn > 0.0, centre - before, after - centre)
        )
        return ocean[:, at] * (centre - change)

    def middle(step, part, halves=(0, 1, 2, 3)):
        lo, hi = span(step, part)

        @pl.loop(lo, hi)
        def _(e):
            for piece in range(halves[0], halves[-1] + 1):
                at = slice(piece * PIECE, (piece + 1) * PIECE)
                new = advanced(step, e, piece)
                state[step + 1, e, :, at] = new
                rows_out[step + 1, 0, e, :, at] = new[ROWS - 1 :, :]
                rows_out[step + 1, 1, e, :, at] = new[:1, :]

    def last(part, halves=(0, 1, 2, 3)):
        lo, hi = span(SUBSTEPS - 1, part)

        @pl.loop(lo, hi)
        def _(e):
            for piece in range(halves[0], halves[-1] + 1):
                new = advanced(SUBSTEPS - 1, e, piece)
                for tile in range(PIECE // LANES):
                    col = piece * (PIECE // LANES) + tile
                    first = (col // 4) * ROWS * BLOCK + col % 4
                    send1[pl.ds(first + (e - HALO) * 4, ROWS, stride=BLOCK), :] = (
                        new[:, tile * LANES : (tile + 1) * LANES]
                    )

    def send_blocks(group, lo, hi):
        @pl.loop(0, 16)
        def _(k):
            away = jnp.where(k < 8, PAIRS[group][0], PAIRS[group][1])
            to = ((plane + away) % PLANE) * PLANE + (low + k) % PLANE
            source = send1.at[pl.ds(pl.multiple_of(to * BLOCK + lo * 4, 8), (hi - lo) * 4)]
            target = recv1.at[pl.ds(pl.multiple_of(me * BLOCK + lo * 4, 8), (hi - lo) * 4)]

            @pl.when(to != me)
            def _():
                pltpu.make_async_remote_copy(
                    src_ref=source,
                    dst_ref=target,
                    send_sem=in_send,
                    recv_sem=in_recv,
                    device_id={"comp": to},
                    device_id_type=MESH,
                ).start()

            @pl.when(to == me)
            def _():
                pltpu.make_async_copy(source, target, in_recv).start()

    inner, sides = (0,), (1, 2)
    for step in range(SUBSTEPS - 1):
        for half in range(4):
            finish_rows(step, inner, (half,))
            middle(step, 0, (half,))
            start_rows(step + 1, inner, (half,))
        if step:
            start_dirs(step)
    for half in range(4):
        finish_rows(SUBSTEPS - 1, inner, (half,))
        last(0, (half,))
    send_blocks(0, *INNER)
    for n in range(0, COMPS, LANES):
        pltpu.make_async_copy(interp_any.at[n : n + LANES], interp.at[n : n + LANES], interp_sem).start()
    for side in range(2):
        for n in range(3):
            dir_copy(side, n).wait()
    mask_first(0, HALO)
    mask_first(HALO + OWN, WIDE)

    @pl.when(south)
    def _():
        for which in range(2):
            diagonal_copy(which, 0).wait_recv()
            diagonal_copy(which, 1).wait_send()

    @pl.when(north)
    def _():
        for which in range(2):
            diagonal_copy(which, 1).wait_recv()
            diagonal_copy(which, 0).wait_send()

    for step in range(SUBSTEPS - 1):
        if step:
            finish_rows(step, sides, (0, 1, 2, 3))
        middle(step, 1)
        middle(step, 2)
        start_rows(step + 1, sides, (0, 1, 2, 3))
        send_blocks(step + 1, *INNER)
    finish_rows(SUBSTEPS - 1, sides)
    last(1)
    last(2)
    for group in range(4):
        send_blocks(group, 0, HALO)
        send_blocks(group, OWN - HALO, OWN)
    wait_bytes(interp, interp_sem)

    @pl.loop(0, COMPS // LANES)
    def _(b):
        span = pl.ds(pl.multiple_of(b * LANES, LANES), LANES)
        store_split(0, span, interp[span, :])
        store_split(1, span, interp[:, span].T)

    wait_bytes(recv1, in_recv)

    @pl.loop(0, COMPS // CHUNK)
    def _(c):
        rows = pl.ds(pl.multiple_of(c * CHUNK, 16), CHUNK)
        for q in range(4):
            value = recv1[pl.ds(c * (CHUNK * 4) + q, CHUNK, stride=4), :]
            at = slice(q * LANES, (q + 1) * LANES)
            high = value.astype(bf16)
            points[rows, at] = value
            points_hi[rows, at] = high
            points_lo[rows, at] = (value - high.astype(f32)).astype(bf16)

    my_group = me // PLANE

    def source_chunk(c, drift):
        group = (plane + plane_offset(c)) % PLANE
        rows = pl.ds(pl.multiple_of(group * CHUNK, 16), CHUNK)
        matrix = jnp.concatenate([split[part, rows, :] for part in range(4)], axis=0)
        both = jnp.dot(matrix, points_hi[...], preferred_element_type=f32)
        more = jnp.dot(matrix[: 2 * CHUNK], points_lo[...], preferred_element_type=f32)
        sums = both[: 2 * CHUNK] + (both[2 * CHUNK :] + more)
        forward, backward = sums[:CHUNK], sums[CHUNK:]
        wave = points[rows, :]
        new = wave + 0.5 * (forward * backward - 0.5 * wave * (forward + backward))
        for q in range(4):
            send2[pl.ds(group * (CHUNK * 4) + q, CHUNK, stride=4), :] = new[:, q * LANES : (q + 1) * LANES]

        @pl.loop(0, PLANE)
        def _(e):
            to = group * PLANE + (low + e) % PLANE

            @pl.when(to != me)
            def _():
                pltpu.make_async_remote_copy(
                    src_ref=block_of(send2, to),
                    dst_ref=block_of(recv2, me),
                    send_sem=out_send,
                    recv_sem=out_recv.at[my_group],
                    device_id={"comp": to},
                    device_id_type=MESH,
                ).start()

            @pl.when(to == me)
            def _():
                pltpu.make_async_copy(
                    block_of(send2, me), block_of(recv2, me), out_recv.at[my_group]
                ).start()

        held = weights[rows, :]
        return tuple(
            drift[a] + jnp.sum((held[:, a : a + 1] * new).reshape(CHUNK // 8, 8, POINTS), axis=0) for a in range(2)
        )

    drift = lax.fori_loop(
        0, PLANE, source_chunk, (jnp.zeros((8, POINTS), f32), jnp.zeros((8, POINTS), f32))
    )
    for a in range(2):
        total = jnp.sum(drift[a], axis=0, keepdims=True)
        for q in range(4):
            drift_block[a * 4 + q : a * 4 + q + 1, :] = total[:, q * LANES : (q + 1) * LANES]

    my_drift = drift_all.at[me]

    @pl.loop(1, TILES)
    def _(t):
        pltpu.make_async_remote_copy(
            src_ref=drift_block,
            dst_ref=my_drift,
            send_sem=drift_send,
            recv_sem=drift_recv,
            device_id={"comp": (me + t) % TILES},
            device_id_type=MESH,
        ).start()

    pltpu.make_async_copy(drift_block, my_drift, drift_recv).start()

    wait_bytes(gathered.at[: TILES - 1], cur_send)
    wait_bytes(recv1.at[: (TILES - 1) * BLOCK], in_send)

    @pl.when(north)
    def _():
        beside_copy(0).wait_send()
        beside_copy(1).wait_recv()

    @pl.when(south)
    def _():
        beside_copy(1).wait_send()
        beside_copy(0).wait_recv()

    @pl.loop(0, PLANE)
    def _(n):
        g = (plane + PLANE - plane_offset(n)) % PLANE
        group_rows = pl.ds(pl.multiple_of(g * PLANE * BLOCK, 8), PLANE * BLOCK)
        wait_bytes(recv2.at[group_rows], out_recv.at[g])

        @pl.loop(0, OWN)
        def _(i):
            for q in range(4):
                cols = pl.ds(pl.multiple_of(g * 4 * LANES + q * LANES, LANES), LANES)
                out[i, :, cols] = recv2[pl.ds(g * PLANE * BLOCK + q + i * 4, ROWS, stride=BLOCK), :]

        cols = pl.ds(pl.multiple_of(g * 4 * LANES, LANES), 4 * LANES)
        pltpu.make_async_copy(out.at[:, :, cols], out_any.at[:, :, cols], store_sem).start()

    wait_bytes(drift_all, drift_recv)
    tile = owner[me]
    row1 = lax.broadcasted_iota(jnp.int32, (ROWS, LANES), 0)

    def twice(value, half):
        other = pltpu.roll(value, 64, 1)
        return jnp.where(half == 0, value, other), jnp.where(half == 0, other, value)

    def mask(which_tile, offset):
        at_left, at_right = twice(masks[offset + 1, which_tile // 2], which_tile % 2)
        return jnp.where(left, at_left, at_right)

    own = mask(tile, 0)
    held = cat[...] * own
    west_tile, east_tile = (tile + TILES - 1) % TILES, (tile + 1) % TILES
    held_w = gathered[inverse[west_tile]] * mask(west_tile, 0)
    held_e = gathered[inverse[east_tile]] * mask(east_tile, 0)
    held_s = jnp.where(south, beside[0] * mask(tile, -1), 0.0)
    held_n = jnp.where(north, beside[1] * mask(tile, 1), 0.0)
    west = jnp.where(lane % 64 == 0, pltpu.roll(held_w, 65, 1), pltpu.roll(held, 1, 1))
    east = jnp.where(lane % 64 == 63, pltpu.roll(held_e, 63, 1), pltpu.roll(held, 127, 1))
    below = jnp.where(row1 == 0, pltpu.roll(held_s, 1, 0), pltpu.roll(held, 1, 0))
    above = jnp.where(row1 == ROWS - 1, pltpu.roll(held_n, 7, 0), pltpu.roll(held, 7, 0))
    lap = west + east + below + above - 4.0 * held
    quarter = (tile % 8) // 2
    sums = [jnp.zeros((ROWS, LANES), f32), jnp.zeros((ROWS, LANES), f32)]
    for r in range(ROWS):
        piece = drift_all[(tile // 8) * ROWS + r]
        for a in range(2):
            chosen = jnp.sum(jnp.where(row1 == quarter + 4 * a, piece, 0.0), axis=0, keepdims=True)
            sums[a] = jnp.where(row1 == r, chosen, sums[a])
    eastward, _ = twice(sums[0], tile % 2)
    _, northward = twice(sums[1], tile % 2)
    stokes = jnp.where(left, eastward, northward)
    turn = jnp.where(left, 1.0, -1.0) * coriolis[rows8, :]
    other = pltpu.roll(held + stokes, 64, 1)
    result = own * (held + 0.5 * (turn * other + 0.2 * lap - 0.1 * held))
    ocean_out[0] = result[:, :64]
    ocean_out[1] = result[:, 64:]

    wait_bytes(drift_all.at[: TILES - 1], drift_send)
    wait_bytes(recv2.at[: (TILES - 1) * BLOCK], out_send)
    wait_bytes(out, store_sem)


def tables():
    angles = np.arange(DIRS, dtype=np.float32) * np.float32(2.0 * math.pi / DIRS)
    cosine, sine = np.cos(angles).astype(np.float32), np.sin(angles).astype(np.float32)
    k = np.arange(COMPS)
    scale = (np.float32(0.2) * (k // DIRS + 1).astype(np.float32) / np.float32(FREQ)).astype(np.float32)
    weights = np.stack([scale * cosine[k % DIRS], scale * sine[k % DIRS]], axis=1)
    latitude = -1.2 + 2.4 * (np.arange(TOTAL_ROWS, dtype=np.float32) + np.float32(0.5)) / TOTAL_ROWS
    coriolis = np.broadcast_to(np.sin(latitude.astype(np.float32))[:, None], (TOTAL_ROWS, LANES))
    return cosine, sine, weights.astype(np.float32), coriolis.astype(np.float32)


def local(spectrum, currents, group_courant, refraction, interp, sea_mask, depth_class, owner_map):
    cosine, sine, weights, coriolis = tables()
    index = jnp.arange(TILES, dtype=jnp.int32)
    inverse = jnp.sum(jnp.where(owner_map[None, :] == index[:, None], index[None, :], 0), axis=1)
    vmem, smem = pl.BlockSpec(memory_space=pltpu.VMEM), pl.BlockSpec(memory_space=pltpu.SMEM)
    anywhere = pl.BlockSpec(memory_space=pl.ANY)
    dma = pltpu.SemaphoreType.DMA
    field = pltpu.VMEM((ROWS, LON), f32)
    blocks = pltpu.VMEM((TILES * BLOCK, LANES), f32)
    edge_rows = pltpu.VMEM((SUBSTEPS, 2, WIDE, 1, LON), f32)
    return pl.pallas_call(
        wave_kernel,
        out_shape=(
            jax.ShapeDtypeStruct((OWN, ROWS, LON), f32),
            jax.ShapeDtypeStruct((2, ROWS, LON // TILES), f32),
        ),
        in_specs=[anywhere, vmem, vmem, vmem, anywhere, vmem, vmem] + [smem] * 6,
        out_specs=(anywhere, vmem),
        scratch_shapes=[
            pltpu.VMEM((SUBSTEPS, WIDE, ROWS, LON), f32),
            edge_rows,
            edge_rows,
            field,
            field,
            field,
            field,
            blocks,
            blocks,
            blocks,
            blocks,
            pltpu.VMEM((OWN, ROWS, LON), f32),
            pltpu.VMEM((COMPS, COMPS), f32),
            pltpu.VMEM((4, COMPS, COMPS), bf16),
            pltpu.VMEM((COMPS, POINTS), f32),
            pltpu.VMEM((COMPS, POINTS), bf16),
            pltpu.VMEM((COMPS, POINTS), bf16),
            pltpu.VMEM((ROWS, LANES), f32),
            pltpu.VMEM((TILES, ROWS, LANES), f32),
            pltpu.VMEM((2, ROWS, LANES), f32),
            pltpu.VMEM((8, LANES), f32),
            pltpu.VMEM((TILES, 8, LANES), f32),
            pltpu.VMEM((3, LON // LANES, ROWS, LANES), f32),
            dma,
            dma,
            dma,
            dma,
            dma((2,)),
            dma((2,)),
            dma((SUBSTEPS, 3, 4, 2)),
            dma((SUBSTEPS, 3, 4, 2)),
            dma((2, 3)),
            dma((2, 3)),
            dma,
            dma,
            dma,
            dma((PLANE,)),
            dma,
            dma,
            dma,
        ],
        compiler_params=pltpu.CompilerParams(
            collective_id=0, has_side_effects=True, vmem_limit_bytes=62 * 2**20
        ),
        name="waves",
    )(
        spectrum, currents, sea_mask, depth_class, interp, jnp.asarray(weights), jnp.asarray(coriolis), group_courant,
        refraction, owner_map, inverse, jnp.asarray(cosine), jnp.asarray(sine),
    )


def solution(mesh):
    in_specs = (P("comp", "band", None), P(None, "band", "comp"), P(), P(), P(), P(), P(), P())
    out_specs = (P("comp", "band", None), P(None, "band", "comp"))
    return jax.shard_map(local, mesh=mesh, in_specs=in_specs, out_specs=out_specs, check_vma=False)
```
